128 devices in a mesh: seq: 16 (over z, x), exp: 8 (over y, core).
Axes of the slice: x: 4, y: 4, z: 4, core: 2. Of those that a mesh axis runs over, the one named last changes fastest.
Arguments:
- query_states: bfloat16 [8, 2048, 4096], P('exp', 'seq'), may hold values from -8 to 8
- key_states: bfloat16 [8, 2048, 1024], P('exp', 'seq'), may hold values from -8 to 8
- value_states: bfloat16 [8, 2048, 1024], P('exp', 'seq'), may hold values from -6 to 6
- residual: bfloat16 [8, 2048, 3072], P('exp', 'seq'), may hold values from -6 to 6
- out_proj: bfloat16 [4096, 3072], P('seq'), may hold values from -0.09375 to 0.09375
- norm_gain: float32 [3072], replicated, may hold values from 0.25 to 1.75
- router: float32 [3072, 8], replicated, may hold values from -0.21875 to 0.21875
- w_gate: bfloat16 [8, 3072, 8192], P('exp', None, 'seq'), may hold values from -0.109375 to 0.109375
- w_up: bfloat16 [8, 3072, 8192], P('exp', None, 'seq'), may hold values from -0.109375 to 0.109375
- w_down: bfloat16 [8, 8192, 3072], P('exp', 'seq'), may hold values from -0.0625 to 0.0625
- reward_head: float32 [3072], replicated, may hold values from -5 to 5
- lengths: int32 [8, 2], P('exp'), may hold values from 512 to 1536, as said below
- routes: int32 [8, 2048, 2], P('exp', 'seq'), may hold values from 0 to 7, all different within a row; in each aligned block of 128 rows (0 to 127, 128 to 255, ..., all dimensions but the last counted through in order) at most 34 rows name the same one
- pair_list: int32 [8, 4, 2], replicated, may hold values from 0 to 1, as said below
Outputs:
- rewards: float32 [8, 2], replicated
- pair_loss: float32 [], replicated
- grad_head: float32 [3072], replicated
- grad_down: bfloat16 [8, 8192, 3072], P('exp', 'seq')
The draws below stay inside these ranges and needn't reach their ends.
Inputs may be any that keep to these rules, and one draw needn't show every extreme that they name: Each group's lengths sum to 2048. `routes`: within the 128 tokens of one device (aligned blocks), each expert is named by at most 34 tokens, a bound that some block reaches; a token's two experts differ. `pair_list`: each judgment names two different responses of its group.
All inputs are finite; a program needn't handle non-finite values.
Results may differ from the reference program's by a relative error of at most 0.023.
Values may be sent and summed in bfloat16 or wider, within the bound.
A program may use at most 192 MiB of HBM per device.

```python
import math
import jax
import jax.numpy as jnp
import numpy as np
from jax import lax

D = 3072
Q_HEADS = 32
KV_HEADS = 8
HEAD_DIM = 128
TOK_DEV = 128
SEQS = 2
PAIRS = 4
EXPERTS = 8
STREAMS = 8
SLEN = 2048
FFW = 8192
CAP = 34
N_SEQ = 16
N_EXP = 8


def common_field(key):
    base_field = jax.random.normal(jax.random.fold_in(key, 101), (STREAMS, SLEN, KV_HEADS, HEAD_DIM), jnp.float32)
    return jnp.clip(base_field, -6.0, 6.0)


def draw_key_states(key, part):
    base_field = common_field(key)
    states = base_field
    return states.reshape(STREAMS, SLEN, KV_HEADS * HEAD_DIM).astype(jnp.bfloat16)


def draw_query_states(key, part):
    key = jax.random.fold_in(key, 9)
    states = jnp.clip(jax.random.normal(key, (STREAMS, SLEN, Q_HEADS, HEAD_DIM), jnp.float32), -6.0, 6.0)
    return states.reshape(STREAMS, SLEN, Q_HEADS * HEAD_DIM).astype(jnp.bfloat16)


def draw_lengths(key, part):
    key = jax.random.fold_in(key, 11)
    first = jax.random.randint(jax.random.fold_in(key, 1), (STREAMS,), SLEN // 4, 3 * SLEN // 4 + 1)
    chosen_group = jax.random.randint(jax.random.fold_in(key, 2), (), 0, STREAMS)
    first = jnp.where(jnp.arange(STREAMS) == chosen_group, 3 * SLEN // 4, first)
    flip = jax.random.randint(jax.random.fold_in(key, 3), (STREAMS,), 0, 2)
    leading = jnp.where(flip == 1, SLEN - first, first)
    return jnp.stack([leading, SLEN - leading], axis=1).astype(jnp.int32)


def draw_pair_list(key, part):
    key = jax.random.fold_in(key, 5)
    chosen = jax.random.randint(jax.random.fold_in(key, 1), (STREAMS, PAIRS), 0, SEQS)
    offset = jax.random.randint(jax.random.fold_in(key, 2), (STREAMS, PAIRS), 1, SEQS)
    rejected = (chosen + offset) % SEQS
    return jnp.stack([chosen, rejected], axis=2).astype(jnp.int32)


def shard_levels(own_key, extent, pieces, low, high):
    def one(axis_at, blocks):
        heights = jax.random.uniform(jax.random.fold_in(jax.random.fold_in(own_key, 6), axis_at), (blocks,), jnp.float32, low / len(pieces), high / len(pieces))
        return jnp.repeat(jnp.exp(heights), extent[axis_at] // blocks).reshape((-1,) + (1,) * (len(extent) - axis_at - 1))

    level = one(*pieces[0])
    for cut in pieces[1:]:
        level = level * one(*cut)
    return level


def shared_out(own_key, own, number, rows, number_of, top, bound, slope):
    order = jax.random.permutation(own_key, number_of)
    packed, common = portions_of(number_of, rows * top, bound, slope, True), portions_of(number_of, rows * top, bound, slope, False)
    places = jnp.arange(number_of)

    def named(sizes, turn):
        used = int((sizes > 0).sum())
        fixed = max(1, used // 4)
        passed = fixed + (places - fixed + turn * (used - fixed)) % max(1, number_of - fixed)
        return jnp.zeros((number_of,), jnp.int32).at[order[jnp.where(places < fixed, places, passed)]].set(jnp.asarray(sizes, jnp.int32))

    sizes = jnp.where(number % 4 == 0, named(packed, number // 4), named(common, number - number // 4 - 1))
    mixed = jax.random.permutation(jax.random.fold_in(own, 3), number_of)
    source_of, sink = mixed[0:number_of // 2 * 2:2], mixed[1:number_of // 2 * 2:2]
    room = jnp.minimum(sizes[source_of] - 1, bound - sizes[sink]) // 2
    room = jnp.where((source_of == order[0]) | (sink == order[0]) | (sizes[sink] == 0), 0, jnp.maximum(room, 0))
    passed = jax.random.randint(jax.random.fold_in(own, 4), (number_of // 2,), 0, 1 << 20) % (room + 1)
    sizes = sizes.at[source_of].add(-passed).at[sink].add(passed)
    items = jnp.searchsorted(jnp.cumsum(sizes), jnp.arange(rows * top), side="right").astype(jnp.int32)
    grid = items.reshape(top, rows).T
    grid = grid[jax.random.permutation(jax.random.fold_in(own, 1), rows)]
    turn = jax.random.randint(jax.random.fold_in(own, 2), (rows, 1), 0, top)
    return jnp.take_along_axis(grid, (jnp.arange(top)[None, :] + turn) % top, axis=1)


def portions_of(count, total, bound, skew, full):
    weights = [(1 << 20) // math.isqrt(grade ** skew) + 1 for grade in range(1, count + 1)]
    largest = bound if full else min(bound, max(-(-total // count), total * weights[0] // sum(weights)))
    least = 1 if total - largest >= count - 1 else 0
    holding, spare = [largest] + [least] * (count - 1), total - largest - least * (count - 1)
    while spare > 0:
        movable = [i for i in range(1, count) if holding[i] < largest] or [i for i in range(1, count) if holding[i] < bound]
        whole, budget = sum([weights[i] for i in movable]), spare
        for i in movable:
            more = min(bound - holding[i], max(1, budget * weights[i] // whole), spare)
            holding[i] = holding[i] + more
            spare = spare - more
    return np.array(holding)


def gaussian(own_key, extent, deviation, most, cuts=(), kind=jnp.bfloat16):
    entries = jax.random.normal(own_key, extent, jnp.float32) * deviation
    if len(cuts) > 0:
        entries = shard_levels(own_key, extent, cuts, -0.22, 0.18) * entries
    return jnp.clip(entries, min=-most, max=most).astype(kind)


def setup_inputs(seed: int = 0) -> dict:
    seeds = jax.random.split(jax.random.key(seed), 15)
    query_states = draw_query_states(jax.random.fold_in(seeds[14], 71), 0)
    key_states = draw_key_states(jax.random.fold_in(seeds[14], 71), 0)
    value_states = gaussian(seeds[2], (STREAMS, SLEN, KV_HEADS * HEAD_DIM), 1.0, 6.0, ((0, 8), (1, 16)))
    residual = gaussian(seeds[3], (STREAMS, SLEN, D), 1.0, 6.0, ((0, 8), (1, 16)))
    out_proj = gaussian(seeds[4], (Q_HEADS * HEAD_DIM, D), (Q_HEADS * HEAD_DIM) ** -0.5, 0.09375, ((0, 16),))
    norm_gain = jnp.clip(1.0 + 0.15 * jax.random.normal(seeds[5], (D,), jnp.float32), 0.25, 1.75)
    router = gaussian(seeds[6], (D, EXPERTS), (D // 4) ** -0.5, 0.21875, (), jnp.float32)
    w_gate = gaussian(seeds[7], (EXPERTS, D, FFW), D ** -0.5, 0.109375, ((0, 8), (2, 16)))
    w_up = gaussian(seeds[8], (EXPERTS, D, FFW), D ** -0.5, 0.109375, ((0, 8), (2, 16)))
    w_down = gaussian(seeds[9], (EXPERTS, FFW, D), FFW ** -0.5, 0.0625, ((0, 8), (1, 16)))
    reward_head = gaussian(seeds[10], (D,), 1.0, 5.0, (), jnp.float32)
    lengths = draw_lengths(jax.random.fold_in(seeds[14], 71), 0)
    routes_keys = jax.random.split(jax.random.fold_in(seeds[12], 1), STREAMS * SLEN // TOK_DEV)
    routes_turns = jax.random.permutation(jax.random.fold_in(seeds[12], 3), STREAMS * SLEN // TOK_DEV)
    routes = jax.vmap(lambda own, number: shared_out(jax.random.fold_in(seeds[12], 2), own, number, TOK_DEV, EXPERTS, 2, CAP, 1))(routes_keys, routes_turns).reshape((STREAMS, SLEN, 2))
    pair_list = draw_pair_list(jax.random.fold_in(seeds[14], 71), 0)
    return {"query_states": query_states, "key_states": key_states, "value_states": value_states, "residual": residual, "out_proj": out_proj, "norm_gain": norm_gain, "router": router, "w_gate": w_gate, "w_up": w_up, "w_down": w_down, "reward_head": reward_head, "lengths": lengths, "routes": routes, "pair_list": pair_list}


def segment_ids(lengths):
    boundary = jnp.cumsum(lengths, axis=1)
    position = jnp.arange(SLEN, dtype=jnp.int32)
    return lax.optimization_barrier(jnp.sum((position[None, :, None] >= boundary[:, None, :]).astype(jnp.int32), axis=2))

def attend_stream(operands):
    query_rows, key_rows, value_rows, segment = operands
    position = jnp.arange(SLEN, dtype=jnp.int32)
    allowed = jnp.logical_and(position[:, None] >= position[None, :], segment[:, None] == segment[None, :])
    group_size = Q_HEADS // KV_HEADS
    query_heads = query_rows.reshape(SLEN, Q_HEADS, HEAD_DIM).transpose(1, 0, 2)
    key_heads = jnp.repeat(key_rows.reshape(SLEN, KV_HEADS, HEAD_DIM), group_size, axis=1).transpose(1, 0, 2)
    value_heads = jnp.repeat(value_rows.reshape(SLEN, KV_HEADS, HEAD_DIM), group_size, axis=1).transpose(1, 0, 2)

    def one_head(triple):
        query_one, key_one, value_one = triple
        scores = jnp.dot(query_one, key_one.T, preferred_element_type=jnp.float32) * HEAD_DIM ** (-0.5)
        scores = jnp.where(allowed, scores, -1e+30)
        largest = lax.optimization_barrier(jnp.max(scores, axis=1, keepdims=True))
        exponent = jnp.exp(scores - largest)
        weights = (exponent / lax.optimization_barrier(jnp.sum(exponent, axis=1, keepdims=True))).astype(jnp.bfloat16)
        return jnp.dot(weights, value_one, preferred_element_type=jnp.float32).astype(jnp.bfloat16)
    heads_out = lax.map(one_head, (query_heads, key_heads, value_heads))
    return heads_out.transpose(1, 0, 2).reshape(SLEN, Q_HEADS * HEAD_DIM)

def reference(query_states, key_states, value_states, residual, out_proj, norm_gain, router, w_gate, w_up, w_down, reward_head, lengths, routes, pair_list):
    highest = lax.Precision.HIGHEST
    segment = segment_ids(lengths)
    attended = lax.map(attend_stream, (query_states, key_states, value_states, segment))
    flat_attn = attended.reshape(STREAMS * SLEN, Q_HEADS * HEAD_DIM)
    width_dev = Q_HEADS * HEAD_DIM // N_SEQ

    def add_group(index, running):
        offset = index.astype(jnp.int32) * width_dev
        columns = lax.dynamic_slice_in_dim(flat_attn, offset, width_dev, 1)
        weight_rows = lax.dynamic_slice_in_dim(out_proj, offset, width_dev, 0)
        part_sum = jnp.dot(columns, weight_rows, preferred_element_type=jnp.float32).astype(jnp.bfloat16)
        return running + lax.optimization_barrier(part_sum).astype(jnp.float32)
    mixed = lax.fori_loop(0, N_SEQ, add_group, jnp.zeros((STREAMS * SLEN, D), jnp.float32))
    hidden_in = residual.reshape(STREAMS * SLEN, D).astype(jnp.float32) + mixed
    scale_row = lax.rsqrt(lax.optimization_barrier(jnp.mean(hidden_in * hidden_in, axis=1, keepdims=True)) + 1e-05)
    normed = (hidden_in * scale_row * norm_gain[None, :]).astype(jnp.bfloat16)
    logits = jnp.dot(normed.astype(jnp.float32), router, precision=highest)
    route_flat = routes.reshape(STREAMS * SLEN, 2)
    first_logit = jnp.take_along_axis(logits, route_flat[:, 0:1], axis=1)[:, 0]
    second_logit = jnp.take_along_axis(logits, route_flat[:, 1:2], axis=1)[:, 0]
    gate_first = jax.nn.sigmoid(first_logit - second_logit)
    gate_second = jax.nn.sigmoid(second_logit - first_logit)
    stream_of = jnp.arange(STREAMS * SLEN, dtype=jnp.int32) // SLEN
    segment_flat = segment.reshape(-1)
    own_length = jnp.take_along_axis(lengths[stream_of], segment_flat[:, None], axis=1)[:, 0].astype(jnp.float32)
    slot_weight = jnp.stack([gate_first / own_length, gate_second / own_length], axis=1).astype(jnp.bfloat16).reshape(-1)
    bucket = stream_of * SEQS + segment_flat
    buckets = STREAMS * SEQS
    bucket_range = jnp.arange(buckets, dtype=jnp.int32)
    pool_rows = (bucket[:, None] == bucket_range[None, :]).astype(jnp.float32) / own_length[:, None]
    pooled_res = jnp.dot(pool_rows.T, hidden_in, precision=highest)
    expert_flat = route_flat.reshape(-1)
    count_all = STREAMS * SLEN * 2
    assign_hot = (expert_flat[:, None] == jnp.arange(EXPERTS, dtype=jnp.int32)[None, :]).astype(jnp.int32)
    slot_rank = lax.optimization_barrier(jnp.sum((jnp.cumsum(assign_hot, axis=0) - 1) * assign_hot, axis=1)).astype(jnp.int32)
    most_rows = CAP * N_SEQ * N_EXP
    slot_table = jnp.zeros((EXPERTS, most_rows), jnp.int32).at[expert_flat, slot_rank].set(jnp.arange(count_all, dtype=jnp.int32))
    present = jnp.zeros((EXPERTS, most_rows), jnp.float32).at[expert_flat, slot_rank].set(1.0)
    token_of = jnp.arange(count_all, dtype=jnp.int32) // 2
    bucket_of = bucket[token_of]

    def expert_pass(operands):
        index_row, present_row, gate_cols, up_cols, down_rows = operands
        gathered = normed[token_of[index_row]]
        gate_vals = jnp.dot(gathered, gate_cols, preferred_element_type=jnp.float32)
        up_vals = jnp.dot(gathered, up_cols, preferred_element_type=jnp.float32)
        activity = jax.nn.silu(gate_vals) * up_vals
        coefficient = slot_weight[index_row].astype(jnp.float32) * present_row
        spread = (bucket_of[index_row][:, None] == bucket_range[None, :]).astype(jnp.float32) * coefficient[:, None]
        summed = jnp.dot(spread.T, activity, precision=highest)
        moved = jnp.dot(summed, down_rows.astype(jnp.float32), precision=highest)
        return (summed, moved)
    hidden_sums, moved_all = lax.map(expert_pass, (slot_table, present, w_gate, w_up, w_down))
    pooled = pooled_res + lax.optimization_barrier(jnp.sum(moved_all, axis=0))
    rewards = jnp.dot(pooled, reward_head, precision=highest).reshape(STREAMS, SEQS)
    chosen_index = pair_list[:, :, 0]
    rejected_index = pair_list[:, :, 1]
    margin = jnp.take_along_axis(rewards, chosen_index, axis=1) - jnp.take_along_axis(rewards, rejected_index, axis=1)
    pair_loss = jnp.mean(jnp.logaddexp(0.0, -margin))
    factor = -jax.nn.sigmoid(-margin) / (STREAMS * PAIRS)
    response_range = jnp.arange(SEQS, dtype=jnp.int32)
    pick_hot = (chosen_index[:, :, None] == response_range).astype(jnp.float32) - (rejected_index[:, :, None] == response_range).astype(jnp.float32)
    reward_grad = lax.optimization_barrier(jnp.sum(factor[:, :, None] * pick_hot, axis=1)).reshape(-1)
    grad_head = jnp.dot(reward_grad, pooled, precision=highest)
    weighted = jnp.einsum('b,ebf->ef', reward_grad, hidden_sums, precision=highest)
    grad_down = (weighted[:, :, None] * reward_head[None, None, :]).astype(jnp.bfloat16)
    return (rewards, pair_loss, grad_head, grad_down)
```

```python
import functools

import jax
import jax.numpy as jnp
from jax import lax
from jax.experimental import pallas as pl
from jax.experimental.pallas import tpu as pltpu
from jax.sharding import PartitionSpec as P

D = 3072
HALF = D // 2
EXT = 128
WIDE = D + EXT
Q_HEADS = 32
KV_HEADS = 8
HEAD_DIM = 128
SEQS = 2
TOK = 128
EXPERTS = 8
CAP = 34
ROWS = EXPERTS * CAP
MAIN = 32
REST = ROWS - EXPERTS * MAIN
NEG = -1e30
F32 = jnp.float32
BF16 = jnp.bfloat16
MESH = pl.DeviceIdType.MESH
VMEM_LIMIT = 60 * 1024 * 1024


def place():
    s = lax.axis_index("seq")
    e = lax.axis_index("exp")
    return s // 4, s % 4, e


def greet(devices):
    barrier = pltpu.get_barrier_semaphore()
    for device in devices:
        pl.semaphore_signal(barrier, inc=1, device_id=device, device_id_type=MESH)
    pl.semaphore_wait(barrier, len(devices))


def remote(src, dst, send, recv, device):
    return pltpu.make_async_remote_copy(
        src_ref=src, dst_ref=dst, send_sem=send, recv_sem=recv, device_id=device, device_id_type=MESH
    )


def lhs_t(a, b):
    return lax.dot_general(a, b, (((0,), (0,)), ((), ())), preferred_element_type=F32)


def rhs_t(a, b):
    return lax.dot_general(a, b, (((1,), (1,)), ((), ())), preferred_element_type=F32)


def mm(a, b):
    return jnp.dot(a, b, preferred_element_type=F32)


def attn_kernel(len_ref, q_ref, k_ref, v_ref, o_ref, qb, kb, vb, lsem, zs, zr, xs, xr):
    z, x, e = place()
    at = lambda zz, xx: (zz * 4 + xx, e)
    greet([at((z + d) % 4, x) for d in (1, 2, 3)] + [at(z, (x + 1) % 4), at(z, (x + 3) % 4)])
    mine = pl.ds(pl.multiple_of(x * TOK, TOK), TOK)
    cols_k = lambda zz: pl.ds(pl.multiple_of(zz * 256, 256), 256)
    cols_q = lambda zz: pl.ds(pl.multiple_of(zz * 1024, 1024), 1024)

    kv_z, q_z = [], []
    for d in (1, 2, 3):
        zt = (z + d) % 4
        to = at(zt, x)
        kv_z.append(
            (
                remote(k_ref.at[:, cols_k(zt)], kb.at[z, mine], zs.at[0, d - 1], zr.at[0, d - 1], to),
                remote(v_ref.at[:, cols_k(zt)], vb.at[z, mine], zs.at[1, d - 1], zr.at[1, d - 1], to),
            )
        )
        q_z.append(remote(q_ref.at[:, cols_q(zt)], qb.at[z], zs.at[2, d - 1], zr.at[2, d - 1], to))
    for d in (2, 1, 3):
        for copy in kv_z[d - 1]:
            copy.start()
    local = [
        pltpu.make_async_copy(k_ref.at[:, cols_k(z)], kb.at[z, mine], lsem.at[0]),
        pltpu.make_async_copy(v_ref.at[:, cols_k(z)], vb.at[z, mine], lsem.at[1]),
        pltpu.make_async_copy(q_ref.at[:, cols_q(z)], qb.at[z], lsem.at[2]),
    ]
    for copy in local:
        copy.start()
    for d in (2, 1, 3):
        q_z[d - 1].start()
    local[0].wait()
    local[1].wait()

    plus, minus = (x + 1) % 4, (x + 3) % 4
    rows = lambda xx: pl.ds(pl.multiple_of(xx * TOK, TOK), TOK)
    near, far = [], []
    for d in (0, 1, 2, 3):
        zz = (z + 4 - d) % 4
        near.append(
            [
                remote(kb.at[zz, mine], kb.at[zz, mine], xs.at[0, d], xr.at[0, d], at(z, plus)),
                remote(vb.at[zz, mine], vb.at[zz, mine], xs.at[1, d], xr.at[1, d], at(z, plus)),
                remote(kb.at[zz, mine], kb.at[zz, mine], xs.at[2, d], xr.at[2, d], at(z, minus)),
                remote(vb.at[zz, mine], vb.at[zz, mine], xs.at[3, d], xr.at[3, d], at(z, minus)),
            ]
        )
        left, right = rows(minus), rows(plus)
        far.append(
            [
                remote(kb.at[zz, left], kb.at[zz, left], xs.at[4, d], xr.at[4, d], at(z, plus)),
                remote(vb.at[zz, right], vb.at[zz, right], xs.at[5, d], xr.at[5, d], at(z, minus)),
            ]
        )
    order = (0, 1, 3, 2)
    for d in order:
        if d:
            kv_z[d - 1][0].wait_recv()
            kv_z[d - 1][1].wait_recv()
        for copy in near[d]:
            copy.start()
    for d in order:
        near[d][0].wait_recv()
        far[d][0].start()
        near[d][3].wait_recv()
        far[d][1].start()
    local[2].wait()
    for d in (1, 3, 2):
        q_z[d - 1].wait_recv()
    for d in order:
        near[d][1].wait_recv()
        near[d][2].wait_recv()
        far[d][0].wait_recv()
        far[d][1].wait_recv()

    bound = len_ref[0, 0]
    scale = HEAD_DIM ** (-0.5) * 1.4426950408889634

    def query_step(zq, _):
        q_all = qb[zq]
        stacked = [
            jnp.concatenate(
                [q_all[:, (4 * h + j) * 128 : (4 * h + j + 1) * 128] for j in range(4)], axis=0
            )
            for h in range(2)
        ]
        qpos = (zq * 4 + x) * TOK + lax.broadcasted_iota(jnp.int32, (TOK, 512), 0)
        first = jnp.where(qpos >= bound, bound, 0)

        def key_step(kz, carry):
            kpos = kz * 512 + lax.broadcasted_iota(jnp.int32, (TOK, 512), 1)
            bias = jnp.where(jnp.logical_and(kpos <= qpos, kpos >= first), 0.0, NEG)
            out = []
            for h in range(2):
                m, l, acc = carry[h]
                sc = rhs_t(stacked[h], kb[kz, :, h * 128 : (h + 1) * 128])
                sc = (sc.reshape(4, TOK, 512) + bias[None]).reshape(512, 512)
                mn = jnp.maximum(m, jnp.max(sc, axis=1, keepdims=True))
                p = jnp.exp2((sc - mn) * scale)
                a = jnp.exp2((m - mn) * scale)
                l = a * l + jnp.sum(p, axis=1, keepdims=True)
                acc = a * acc + mm(p.astype(BF16), vb[kz, :, h * 128 : (h + 1) * 128])
                out.append((mn, l, acc))
            return tuple(out)

        start = (
            jnp.full((512, 1), NEG, F32),
            jnp.zeros((512, 1), F32),
            jnp.zeros((512, 128), F32),
        )
        done = lax.fori_loop(0, zq + 1, key_step, (start, start))
        for h in range(2):
            _, l, acc = done[h]
            res = (acc / l).astype(BF16)
            for j in range(4):
                o_ref[zq, :, (4 * h + j) * 128 : (4 * h + j + 1) * 128] = res[j * 128 : (j + 1) * 128]
        return 0

    lax.fori_loop(0, 4, query_step, 0)
    for d in range(3):
        kv_z[d][0].wait_send()
        kv_z[d][1].wait_send()
        q_z[d].wait_send()
    for d in range(4):
        for copy in near[d] + far[d]:
            copy.wait_send()


def attention(lengths, q, k, v):
    any_spec = pl.BlockSpec(memory_space=pl.ANY)
    return pl.pallas_call(
        attn_kernel,
        out_shape=jax.ShapeDtypeStruct((4, TOK, 1024), BF16),
        in_specs=[pl.BlockSpec(memory_space=pltpu.SMEM), any_spec, any_spec, any_spec],
        out_specs=pl.BlockSpec(memory_space=pltpu.VMEM),
        scratch_shapes=[
            pltpu.VMEM((4, TOK, 1024), BF16),
            pltpu.VMEM((4, 512, 256), BF16),
            pltpu.VMEM((4, 512, 256), BF16),
            pltpu.SemaphoreType.DMA((3,)),
            pltpu.SemaphoreType.DMA((3, 3)),
            pltpu.SemaphoreType.DMA((3, 3)),
            pltpu.SemaphoreType.DMA((6, 4)),
            pltpu.SemaphoreType.DMA((6, 4)),
        ],
        compiler_params=pltpu.CompilerParams(
            collective_id=0, has_side_effects=True, vmem_limit_bytes=VMEM_LIMIT
        ),
        cost_estimate=pl.CostEstimate(
            flops=4_000_000_000, bytes_accessed=4_000_000, transcendentals=5_000_000
        ),
        name="attention",
    )(lengths, q, k, v)


def moe_kernel(
    len_ref, att, wz, res, gain, router, routes, wg_hbm, wu_hbm,
    hs_out, pool_out,
    part, rs, hid, nrm, stage, pack, unpack, xb, wg, wu, hs, hr,
    rs_s, rs_r, w_s, w_r, y_s, y_r, z_s, z_r, x_s, x_r, h_s, h_r, lsem,
):
    z, x, e = place()
    core = e % 2
    swap, flip = x + 1 - 2 * (x % 2), 3 - x
    x_weight = swap * (1 - core) + flip * core
    x_token = flip * (1 - core) + swap * core
    at = lambda zz, xx, ee: (zz * 4 + xx, ee)
    zp, zm = at((z + 1) % 4, x, e), at((z + 3) % 4, x, e)
    partner_w, partner_t = at(z, x_weight, e), at(z, x_token, e)
    greet([at(z, x, (e + d) % 8) for d in range(1, 8)] + [zp, zm, partner_w, partner_t])

    own_w, far_w = [], []
    for c in range(2):
        cols = pl.ds(c * 256, 256)
        for i, (hbm, buf) in enumerate(((wg_hbm, wg), (wu_hbm, wu))):
            own_w.append(pltpu.make_async_copy(hbm.at[:, cols], buf.at[c], lsem.at[2 * c + i]))
            far_w.append(
                remote(hbm.at[:, cols], buf.at[2 + c], w_s.at[2 * c + i], w_r.at[2 * c + i], partner_w)
            )

    def project(target, half):
        return mm(att[target], wz[:, half * HALF : (half + 1) * HALF])

    z2, z1, z3 = (z + 2) % 4, (z + 1) % 4, (z + 3) % 4
    rsc = [
        remote(part.at[i], rs.at[i], rs_s.at[i], rs_r.at[i], zp if i % 2 == 0 else zm)
        for i in range(6)
    ]
    part[0] = project(z2, 0).astype(BF16)
    rsc[0].start()
    part[1] = project(z2, 1).astype(BF16)
    rsc[1].start()
    for copy in own_w + far_w:
        copy.start()
    part[2] = project(z1, 1).astype(BF16)
    rsc[2].start()
    part[3] = project(z3, 0).astype(BF16)
    rsc[3].start()
    through_a = project(z1, 0)
    rsc[0].wait_recv()
    part[4] = (through_a + rs[0].astype(F32)).astype(BF16)
    rsc[4].start()
    through_b = project(z3, 1)
    rsc[1].wait_recv()
    part[5] = (through_b + rs[1].astype(F32)).astype(BF16)
    rsc[5].start()
    for half in range(2):
        span = slice(half * HALF, (half + 1) * HALF)
        hid[:, span] = res[:, span].astype(F32) + project(z, half)

    ids = lax.broadcasted_iota(jnp.int32, (TOK, EXPERTS), 1)
    hot = [ids == routes[:, k : k + 1] for k in range(2)]
    named = jnp.where(jnp.logical_or(hot[0], hot[1]), 1.0, 0.0).astype(BF16)
    earlier = jnp.where(
        lax.broadcasted_iota(jnp.int32, (TOK, TOK), 1) < lax.broadcasted_iota(jnp.int32, (TOK, TOK), 0),
        1.0,
        0.0,
    ).astype(BF16)
    before = mm(earlier, named)
    slot_ids = lax.broadcasted_iota(jnp.int32, (TOK, ROWS), 1)
    slot_hot = []
    for k in range(2):
        rank = jnp.sum(jnp.where(hot[k], before, 0.0), axis=1, keepdims=True).astype(jnp.int32)
        expert = routes[:, k : k + 1]
        slot = jnp.where(
            rank < MAIN, expert * MAIN + rank, EXPERTS * MAIN + expert * 2 + (rank - MAIN)
        )
        slot_hot.append(jnp.where(slot_ids == slot, 1.0, 0.0).astype(BF16))
    slot_any = slot_hot[0] + slot_hot[1]
    bound = len_ref[0, 0]
    second = len_ref[0, 1]
    tpos = (z * 4 + x) * TOK + lax.broadcasted_iota(jnp.int32, (TOK, 1), 0)
    in_second = tpos >= bound
    own_len = jnp.where(in_second, second, bound).astype(F32)

    rsc[2].wait_recv()
    rsc[3].wait_recv()
    hid[:, :HALF] = hid[:, :HALF] + rs[3].astype(F32)
    hid[:, HALF:] = hid[:, HALF:] + rs[2].astype(F32)
    rsc[4].wait_recv()
    rsc[5].wait_recv()
    hid[:, :HALF] = hid[:, :HALF] + rs[4].astype(F32)
    hid[:, HALF:] = hid[:, HALF:] + rs[5].astype(F32)

    square = jnp.sum(hid[...] * hid[...], axis=1, keepdims=True) * (1.0 / D)
    norm_scale = lax.rsqrt(square + 1e-05)
    nrm[...] = (hid[...] * norm_scale * gain[...]).astype(BF16)

    r_all = router[...]
    r_hi = r_all.astype(BF16)
    r_rest = r_all - r_hi.astype(F32)
    r_mid = r_rest.astype(BF16)
    r_low = (r_rest - r_mid.astype(F32)).astype(BF16)
    logits = rhs_t(nrm[...], r_hi) + rhs_t(nrm[...], r_mid) + rhs_t(nrm[...], r_low)
    picked = [jnp.sum(jnp.where(hot[k], logits, 0.0), axis=1, keepdims=True) for k in range(2)]
    gates = [
        1.0 / (1.0 + jnp.exp(picked[1] - picked[0])),
        1.0 / (1.0 + jnp.exp(picked[0] - picked[1])),
    ]
    bucket = jnp.where(in_second, 8, 0) + e
    lanes = lax.broadcasted_iota(jnp.int32, (TOK, EXT), 1)
    ext = jnp.zeros((ROWS, EXT), F32)
    for k in range(2):
        weight = (gates[k] / own_len).astype(BF16).astype(F32)
        ext = ext + lhs_t(slot_hot[k], jnp.where(lanes == bucket, weight, 0.0).astype(BF16))
    for c in range(4):
        span = slice(c * 768, (c + 1) * 768)
        stage[:, span] = lhs_t(slot_any, nrm[:, span]).astype(BF16)
    stage[:, D:] = ext.astype(BF16)

    tall = lax.broadcasted_iota(jnp.int32, (TOK, REST), 0)
    wide = lax.broadcasted_iota(jnp.int32, (TOK, REST), 1)
    base = (wide // 2) * 16 + (wide % 2) * 8
    for j in range(4):
        got = jnp.zeros((TOK, 128), F32)
        for kk in range(8):
            chunk = 8 * j + kk
            if chunk * 128 < WIDE:
                pick = jnp.where(tall == base + kk, 1.0, 0.0).astype(BF16)
                got = got + mm(pick, stage[EXPERTS * MAIN :, chunk * 128 : (chunk + 1) * 128])
        pack[:, :, j * 128 : (j + 1) * 128] = got.astype(BF16).reshape(EXPERTS, 16, 128)

    own_slot = 2 * z
    my_rows = pl.ds(pl.multiple_of(e * MAIN, MAIN), MAIN)
    y_copies = []
    for d in range(1, 8):
        et = (e + d) % 8
        to = at(z, x, et)
        y_copies.append(
            remote(
                stage.at[pl.ds(pl.multiple_of(et * MAIN, MAIN), MAIN)],
                xb.at[own_slot, my_rows],
                y_s.at[0, d - 1],
                y_r.at[0, d - 1],
                to,
            )
        )
        y_copies.append(remote(pack.at[et], unpack.at[e], y_s.at[1, d - 1], y_r.at[1, d - 1], to))
    for copy in y_copies:
        copy.start()
    keep = [
        pltpu.make_async_copy(stage.at[my_rows], xb.at[own_slot, my_rows], lsem.at[4]),
        pltpu.make_async_copy(pack.at[e], unpack.at[e], lsem.at[5]),
    ]
    for copy in keep:
        copy.start()

    inv = 1.0 / own_len
    pool_out[...] = jnp.zeros_like(pool_out)
    pool_out[0:1] = jnp.sum(hid[...] * jnp.where(in_second, 0.0, inv), axis=0, keepdims=True)
    pool_out[1:2] = jnp.sum(hid[...] * jnp.where(in_second, inv, 0.0), axis=0, keepdims=True)
    hs[...] = jnp.zeros_like(hs)

    for copy in keep:
        copy.wait()
    for copy in y_copies:
        copy.wait_recv()
    flat = unpack[...].reshape(TOK, 512)
    tall_t = lax.broadcasted_iota(jnp.int32, (REST, TOK), 0)
    wide_t = lax.broadcasted_iota(jnp.int32, (REST, TOK), 1)
    base_t = (tall_t // 2) * 16 + (tall_t % 2) * 8
    for kk in range(8):
        pick = jnp.where(wide_t == base_t + kk, 1.0, 0.0).astype(BF16)
        got = mm(pick, flat).astype(BF16)
        for j in range(4):
            chunk = 8 * j + kk
            if chunk * 128 < WIDE:
                xb[own_slot, EXPERTS * MAIN :, chunk * 128 : (chunk + 1) * 128] = got[
                    :, j * 128 : (j + 1) * 128
                ]

    slot_of = lambda d: 2 * ((z + 4 - d) % 4)
    top, bottom = pl.ds(0, 128), pl.ds(128, ROWS - 128)
    zc = [
        remote(xb.at[own_slot], xb.at[own_slot], z_s.at[0], z_r.at[0], zp),
        remote(xb.at[own_slot], xb.at[own_slot], z_s.at[1], z_r.at[1], zm),
        remote(xb.at[slot_of(1), top], xb.at[slot_of(1), top], z_s.at[2], z_r.at[2], zp),
        remote(xb.at[slot_of(3), bottom], xb.at[slot_of(3), bottom], z_s.at[3], z_r.at[3], zm),
    ]
    xc = [
        remote(xb.at[slot_of(d)], xb.at[slot_of(d) + 1], x_s.at[d], x_r.at[d], partner_t)
        for d in range(4)
    ]
    zc[0].start()
    zc[1].start()
    xc[0].start()

    for copy in own_w + far_w[:0]:
        copy.wait()

    def experts(slot):
        def chunk_step(c, _):
            rows = xb[slot, :, :D]
            gate = mm(rows, wg[c])
            up = mm(rows, wu[c])
            act = (gate / (1.0 + jnp.exp(-gate)) * up).astype(BF16)
            hs[c] = hs[c] + lhs_t(xb[slot, :, D:], act)
            return 0

        lax.fori_loop(0, 4, chunk_step, 0)

    zc[0].wait_recv()
    zc[2].start()
    xc[1].start()
    zc[1].wait_recv()
    zc[3].start()
    xc[3].start()
    for copy in far_w:
        copy.wait_recv()
    experts(own_slot)
    experts(slot_of(1))
    zc[2].wait_recv()
    zc[3].wait_recv()
    xc[2].start()
    experts(slot_of(3))
    xc[0].wait_recv()
    experts(own_slot + 1)
    experts(slot_of(2))
    for d in (1, 3, 2):
        xc[d].wait_recv()
        experts(slot_of(d) + 1)

    home = remote(hs.at[pl.ds(2, 2), pl.ds(0, 16)], hr, h_s, h_r, partner_w)
    home.start()
    home.wait_recv()
    for c in range(2):
        hs_out[:, c * 256 : (c + 1) * 256] = hs[c, 0:16] + hr[c]
    home.wait_send()
    for copy in rsc + far_w + y_copies + zc + xc:
        copy.wait_send()


def moe(lengths, att, wz, res, gain, router_t, routes, w_gate, w_up):
    vmem = pl.BlockSpec(memory_space=pltpu.VMEM)
    hbm = pl.BlockSpec(memory_space=pl.ANY)
    dma = pltpu.SemaphoreType.DMA
    return pl.pallas_call(
        moe_kernel,
        out_shape=(
            jax.ShapeDtypeStruct((16, 512), F32),
            jax.ShapeDtypeStruct((8, D), F32),
        ),
        in_specs=[pl.BlockSpec(memory_space=pltpu.SMEM)] + [vmem] * 6 + [hbm, hbm],
        out_specs=(vmem, vmem),
        scratch_shapes=[
            pltpu.VMEM((6, TOK, HALF), BF16),
            pltpu.VMEM((6, TOK, HALF), BF16),
            pltpu.VMEM((TOK, D), F32),
            pltpu.VMEM((TOK, D), BF16),
            pltpu.VMEM((ROWS, WIDE), BF16),
            pltpu.VMEM((EXPERTS, 16, 512), BF16),
            pltpu.VMEM((EXPERTS, 16, 512), BF16),
            pltpu.VMEM((8, ROWS, WIDE), BF16),
            pltpu.VMEM((4, D, 256), BF16),
            pltpu.VMEM((4, D, 256), BF16),
            pltpu.VMEM((4, EXT, 256), F32),
            pltpu.VMEM((2, 16, 256), F32),
            dma((6,)), dma((6,)),
            dma((4,)), dma((4,)),
            dma((2, 7)), dma((2, 7)),
            dma((4,)), dma((4,)),
            dma((4,)), dma((4,)),
            dma, dma,
            dma((6,)),
        ],
        compiler_params=pltpu.CompilerParams(
            collective_id=1, has_side_effects=True, vmem_limit_bytes=VMEM_LIMIT
        ),
        cost_estimate=pl.CostEstimate(
            flops=32_000_000_000, bytes_accessed=20_000_000, transcendentals=3_000_000
        ),
        name="experts",
    )(lengths, att, wz, res, gain, router_t, routes, w_gate, w_up)


def final_kernel(
    hs, pool, vec, head, wd, chosen, rejected,
    rew_out, loss_out, gh_out, wt_out,
    r_mine, r_exp, r_sum, r_seq, g_mine, g_exp, g_sum, g_seq,
    re_s, re_r, rq_s, rq_r, ge_s, ge_r, gq_s, gq_r,
):
    s = lax.axis_index("seq")
    e = lax.axis_index("exp")
    exp_peers = [(s, (e + d) % 8) for d in range(1, 8)]
    seq_peers = [((s + d) % 16, e) for d in range(1, 16)]
    greet(exp_peers + seq_peers)

    def all_sum(mine, got_exp, total, got_seq, es, er, qs, qr):
        copies = [
            remote(mine, got_exp.at[i], es.at[i], er.at[i], to) for i, to in enumerate(exp_peers)
        ]
        for copy in copies:
            copy.start()
        acc = mine[...]
        for i, copy in enumerate(copies):
            copy.wait_recv()
            acc = acc + got_exp[i]
        total[...] = acc
        more = [
            remote(total, got_seq.at[i], qs.at[i], qr.at[i], to) for i, to in enumerate(seq_peers)
        ]
        for copy in more:
            copy.start()
        for i, copy in enumerate(more):
            copy.wait_recv()
            acc = acc + got_seq[i]
        return acc, copies + more

    hsv = hs[...]
    part = jnp.sum(hsv * vec[...], axis=1, keepdims=True)
    own = jnp.sum(pool[...] * head[...], axis=1, keepdims=True)
    group = lax.broadcasted_iota(jnp.int32, (8, 128), 0)
    r_mine[0:8] = part[0:8] + jnp.where(group == e, own[0:1], 0.0)
    r_mine[8:16] = part[8:16] + jnp.where(group == e, own[1:2], 0.0)
    rewards, sent = all_sum(r_mine, r_exp, r_sum, r_seq, re_s, re_r, rq_s, rq_r)
    rew_out[...] = rewards

    r0, r1 = rewards[0:8], rewards[8:16]
    ch, rj = chosen[...], rejected[...]
    margin = jnp.where(ch == 0, r0, r1) - jnp.where(rj == 0, r0, r1)
    real = lax.broadcasted_iota(jnp.int32, (8, 128), 1) < 4
    loss = jnp.maximum(-margin, 0.0) + jnp.log1p(jnp.exp(-jnp.abs(margin)))
    loss = jnp.sum(jnp.where(real, loss, 0.0), axis=1, keepdims=True)
    loss = jnp.sum(loss, axis=0, keepdims=True) * (1.0 / 32.0)
    loss_out[...] = jnp.broadcast_to(loss, (8, 128))
    factor = jnp.where(real, -1.0 / (1.0 + jnp.exp(margin)) * (1.0 / 32.0), 0.0)
    up0 = jnp.where(ch == 0, factor, 0.0) - jnp.where(rj == 0, factor, 0.0)
    up1 = jnp.where(ch == 1, factor, 0.0) - jnp.where(rj == 1, factor, 0.0)
    rg0 = jnp.sum(up0, axis=1, keepdims=True)
    rg1 = jnp.sum(up1, axis=1, keepdims=True)
    weighted = jnp.sum(hsv[0:8] * rg0 + hsv[8:16] * rg1, axis=0, keepdims=True)
    wt_out[...] = jnp.broadcast_to(weighted, (8, 512))
    hi = weighted.astype(BF16).astype(F32)
    mid = (weighted - hi).astype(BF16).astype(F32)
    low = weighted - hi - mid
    line = lax.broadcasted_iota(jnp.int32, (16, 512), 0)
    three = jnp.where(line == 0, hi, jnp.where(line == 1, mid, jnp.where(line == 2, low, 0.0)))
    moved = jnp.sum(mm(three.astype(BF16), wd[...]), axis=0, keepdims=True)
    mine = lax.broadcasted_iota(jnp.int32, (8, 1), 0) == e
    own0 = jnp.sum(jnp.where(mine, rg0, 0.0), axis=0, keepdims=True)
    own1 = jnp.sum(jnp.where(mine, rg1, 0.0), axis=0, keepdims=True)
    grad = moved + own0 * pool[0:1] + own1 * pool[1:2]
    for i in range(24):
        g_mine[i : i + 1] = grad[:, i * 128 : (i + 1) * 128]
    total, more = all_sum(g_mine, g_exp, g_sum, g_seq, ge_s, ge_r, gq_s, gq_r)
    gh_out[...] = total
    for copy in sent + more:
        copy.wait_send()


def final(hs, pool, vec, head, wd, chosen, rejected):
    vmem = pl.BlockSpec(memory_space=pltpu.VMEM)
    dma = pltpu.SemaphoreType.DMA
    return pl.pallas_call(
        final_kernel,
        out_shape=(
            jax.ShapeDtypeStruct((16, 128), F32),
            jax.ShapeDtypeStruct((8, 128), F32),
            jax.ShapeDtypeStruct((24, 128), F32),
            jax.ShapeDtypeStruct((8, 512), F32),
        ),
        in_specs=[vmem] * 7,
        out_specs=(vmem,) * 4,
        scratch_shapes=[
            pltpu.VMEM((16, 128), F32), pltpu.VMEM((7, 16, 128), F32),
            pltpu.VMEM((16, 128), F32), pltpu.VMEM((15, 16, 128), F32),
            pltpu.VMEM((24, 128), F32), pltpu.VMEM((7, 24, 128), F32),
            pltpu.VMEM((24, 128), F32), pltpu.VMEM((15, 24, 128), F32),
            dma((7,)), dma((7,)), dma((15,)), dma((15,)),
            dma((7,)), dma((7,)), dma((15,)), dma((15,)),
        ],
        compiler_params=pltpu.CompilerParams(
            collective_id=2, has_side_effects=True, vmem_limit_bytes=VMEM_LIMIT
        ),
        name="final",
    )(hs, pool, vec, head, wd, chosen, rejected)


def per_device(
    query_states, key_states, value_states, residual, out_proj, norm_gain, router,
    w_gate, w_up, w_down, reward_head, lengths, routes, pair_list,
):
    columns = [[4 * z + x for x in range(4)] for z in range(4)]
    wz = lax.all_gather(out_proj, "seq", axis=0, tiled=True, axis_index_groups=columns)
    att = attention(lengths, query_states[0], key_states[0], value_states[0])
    vec = jnp.sum(w_down[0].astype(F32) * reward_head[None, :], axis=1)[None, :]
    hs, pool = moe(
        lengths, att, wz, residual[0], norm_gain[None, :], router.T, routes[0], w_gate[0], w_up[0]
    )
    pad = ((0, 0), (0, 124))
    rew, loss, gh, wt = final(
        hs, pool, vec, reward_head[None, :], w_down[0],
        jnp.pad(pair_list[:, :, 0], pad), jnp.pad(pair_list[:, :, 1], pad),
    )
    rewards = rew[:, 0].reshape(2, 8).T
    grad_down = (wt[0][:, None] * reward_head[None, :]).astype(BF16)[None]
    return rewards, loss[0, 0], gh.reshape(-1), grad_down


def solution(mesh):
    placed = (
        P("exp", "seq", None), P("exp", "seq", None), P("exp", "seq", None), P("exp", "seq", None),
        P("seq", None), P(), P(), P("exp", None, "seq"), P("exp", None, "seq"),
        P("exp", "seq", None), P(), P("exp", None), P("exp", "seq", None), P(),
    )
    return jax.shard_map(
        per_device,
        mesh=mesh,
        in_specs=placed,
        out_specs=(P(), P(), P(), P("exp", "seq", None)),
        check_vma=False,
    )
```

```python
import functools

import jax
import jax.numpy as jnp
from jax import lax
from jax.experimental import pallas as pl
from jax.experimental.pallas import tpu as pltpu
from jax.sharding import PartitionSpec as P

D = 3072
BLK = 384
CHUNKS = 4
CW = D // CHUNKS
X_FIRST = (1,)
EXT = 128
WIDE = D + EXT
Q_HEADS = 32
KV_HEADS = 8
HEAD_DIM = 128
SEQS = 2
TOK = 128
EXPERTS = 8
CAP = 34
ROWS = EXPERTS * CAP
MAIN = 32
REST = ROWS - EXPERTS * MAIN
NEG = -1e30
F32 = jnp.float32
BF16 = jnp.bfloat16
MESH = pl.DeviceIdType.MESH
VMEM_LIMIT = 60 * 1024 * 1024


def place():
    s = lax.axis_index("seq")
    e = lax.axis_index("exp")
    return s // 4, s % 4, e


def greet(devices):
    barrier = pltpu.get_barrier_semaphore()
    for device in devices:
        pl.semaphore_signal(barrier, inc=1, device_id=device, device_id_type=MESH)
    pl.semaphore_wait(barrier, len(devices))


def remote(src, dst, send, recv, device):
    return pltpu.make_async_remote_copy(
        src_ref=src, dst_ref=dst, send_sem=send, recv_sem=recv, device_id=device, device_id_type=MESH
    )


def lhs_t(a, b):
    return lax.dot_general(a, b, (((0,), (0,)), ((), ())), preferred_element_type=F32)


def rhs_t(a, b):
    return lax.dot_general(a, b, (((1,), (1,)), ((), ())), preferred_element_type=F32)


def mm(a, b):
    return jnp.dot(a, b, preferred_element_type=F32)


def layer_kernel(
    len_ref, q_ref, k_ref, v_ref, op_ref, res, gain, router, routes, wg_hbm, wu_hbm,
    hs_out, pool_out,
    qb, kb, vb, att, wb, part, rs, hid, nrm, stage, pack, unpack, xb, wg, wu, hs, hr,
    lsem, zs, zr, xs, xr, o_s, o_r, rs_s, rs_r, w_s, w_r, y_s, y_r, z_s, z_r, zd_s, zd_r,
    x_s, x_r, h_s, h_r,
):
    z, x, e = place()
    core = e % 2
    at = lambda zz, xx, ee: (zz * 4 + xx, ee)
    z1, z2, z3 = (z + 1) % 4, (z + 2) % 4, (z + 3) % 4
    plus, across, minus = (x + 1) % 4, (x + 2) % 4, (x + 3) % 4
    swap, flip = x + 1 - 2 * (x % 2), 3 - x
    x_weight = swap * (1 - core) + flip * core
    x_token = flip * (1 - core) + swap * core
    zp, zm = at(z1, x, e), at(z3, x, e)
    xp, xm = at(z, plus, e), at(z, minus, e)
    partner_w, partner_t = at(z, x_weight, e), at(z, x_token, e)
    greet(
        [zp, zm, at(z2, x, e), xp, xm, at(z, across, e)]
        + [at(z, x, (e + d) % 8) for d in range(1, 8)]
    )

    mine = pl.ds(pl.multiple_of(x * TOK, TOK), TOK)
    cols_k = lambda zz: pl.ds(pl.multiple_of(zz * 256, 256), 256)
    cols_q = lambda zz: pl.ds(pl.multiple_of(zz * 1024, 1024), 1024)
    kv_z, q_z = [], []
    for d in (1, 2, 3):
        zt = (z + d) % 4
        to = at(zt, x, e)
        kv_z.append(
            (
                remote(k_ref.at[:, cols_k(zt)], kb.at[z, mine], zs.at[0, d - 1], zr.at[0, d - 1], to),
                remote(v_ref.at[:, cols_k(zt)], vb.at[z, mine], zs.at[1, d - 1], zr.at[1, d - 1], to),
            )
        )
        q_z.append(remote(q_ref.at[:, cols_q(zt)], qb.at[z], zs.at[2, d - 1], zr.at[2, d - 1], to))
    for d in (2, 1, 3):
        for copy in kv_z[d - 1]:
            copy.start()
    own_cols = pl.ds(pl.multiple_of(e * BLK, 128), BLK)
    own_rows = pl.ds(pl.multiple_of(x * 256, 256), 256)
    local = [
        pltpu.make_async_copy(k_ref.at[:, cols_k(z)], kb.at[z, mine], lsem.at[0]),
        pltpu.make_async_copy(v_ref.at[:, cols_k(z)], vb.at[z, mine], lsem.at[1]),
        pltpu.make_async_copy(q_ref.at[:, cols_q(z)], qb.at[z], lsem.at[2]),
        pltpu.make_async_copy(op_ref.at[:, own_cols], wb.at[e, own_rows], lsem.at[3]),
    ]
    for copy in local:
        copy.start()
    w_x = [
        remote(op_ref.at[:, own_cols], wb.at[e, own_rows], o_s.at[i], o_r.at[i], at(z, xx, e))
        for i, xx in enumerate((plus, across, minus))
    ]
    for copy in w_x:
        copy.start()
    for d in (2, 1, 3):
        q_z[d - 1].start()
    local[0].wait()
    local[1].wait()

    rows = lambda xx: pl.ds(pl.multiple_of(xx * TOK, TOK), TOK)
    near, far = [], []
    for d in (0, 1, 2, 3):
        zz = (z + 4 - d) % 4
        near.append(
            [
                remote(kb.at[zz, mine], kb.at[zz, mine], xs.at[0, d], xr.at[0, d], xp),
                remote(vb.at[zz, mine], vb.at[zz, mine], xs.at[1, d], xr.at[1, d], xp),
                remote(kb.at[zz, mine], kb.at[zz, mine], xs.at[2, d], xr.at[2, d], xm),
                remote(vb.at[zz, mine], vb.at[zz, mine], xs.at[3, d], xr.at[3, d], xm),
            ]
        )
        left, right = rows(minus), rows(plus)
        far.append(
            [
                remote(kb.at[zz, left], kb.at[zz, left], xs.at[4, d], xr.at[4, d], xp),
                remote(vb.at[zz, right], vb.at[zz, right], xs.at[5, d], xr.at[5, d], xm),
            ]
        )
    order = (0, 1, 3, 2)
    for d in order:
        if d:
            kv_z[d - 1][0].wait_recv()
            kv_z[d - 1][1].wait_recv()
        for copy in near[d]:
            copy.start()
    y_up, y_down = (e + 2) % 8, (e + 6) % 8
    other = e + 1 - 2 * core
    upper, lower = pl.ds(0, 512), pl.ds(512, 512)
    w_y = [
        remote(wb.at[e], wb.at[e], o_s.at[3], o_r.at[3], at(z, x, y_up)),
        remote(wb.at[e], wb.at[e], o_s.at[4], o_r.at[4], at(z, x, y_down)),
        remote(wb.at[y_down, upper], wb.at[y_down, upper], o_s.at[5], o_r.at[5], at(z, x, y_up)),
        remote(wb.at[y_up, lower], wb.at[y_up, lower], o_s.at[6], o_r.at[6], at(z, x, y_down)),
    ]
    w_c = [
        remote(wb.at[ee], wb.at[ee], o_s.at[7 + i], o_r.at[7 + i], at(z, x, other))
        for i, ee in enumerate((e, y_down, y_up, (e + 4) % 8))
    ]
    local[3].wait()
    for copy in w_x:
        copy.wait_recv()
    w_y[0].start()
    w_y[1].start()
    w_c[0].start()
    for d in order:
        near[d][0].wait_recv()
        far[d][0].start()
        near[d][3].wait_recv()
        far[d][1].start()
    local[2].wait()
    for d in (1, 3, 2):
        q_z[d - 1].wait_recv()
    for d in order:
        near[d][1].wait_recv()
        near[d][2].wait_recv()
        far[d][0].wait_recv()
        far[d][1].wait_recv()

    own_w, far_w = [], []
    for c in range(2):
        cols = pl.ds(c * 256, 256)
        for i, (hbm, buf) in enumerate(((wg_hbm, wg), (wu_hbm, wu))):
            own_w.append(pltpu.make_async_copy(hbm.at[:, cols], buf.at[c], lsem.at[4 + 2 * c + i]))
            far_w.append(
                remote(hbm.at[:, cols], buf.at[2 + c], w_s.at[2 * c + i], w_r.at[2 * c + i], partner_w)
            )
    for copy in far_w + own_w:
        copy.start()

    bound = len_ref[0, 0]
    second = len_ref[0, 1]
    scale = HEAD_DIM ** (-0.5) * 1.4426950408889634

    def query_step(zq, _):
        q_all = qb[zq]
        stacked = [
            jnp.concatenate(
                [q_all[:, (4 * h + j) * 128 : (4 * h + j + 1) * 128] for j in range(4)], axis=0
            )
            for h in range(2)
        ]
        qpos = (zq * 4 + x) * TOK + lax.broadcasted_iota(jnp.int32, (TOK, 512), 0)
        first = jnp.where(qpos >= bound, bound, 0)

        def key_step(kz, carry):
            kpos = kz * 512 + lax.broadcasted_iota(jnp.int32, (TOK, 512), 1)
            bias = jnp.where(jnp.logical_and(kpos <= qpos, kpos >= first), 0.0, NEG)
            out = []
            for h in range(2):
                m, l, acc = carry[h]
                sc = rhs_t(stacked[h], kb[kz, :, h * 128 : (h + 1) * 128])
                sc = (sc.reshape(4, TOK, 512) + bias[None]).reshape(512, 512)
                mn = jnp.maximum(m, jnp.max(sc, axis=1, keepdims=True))
                p = jnp.exp2((sc - mn) * scale)
                a = jnp.exp2((m - mn) * scale)
                l = a * l + jnp.sum(p, axis=1, keepdims=True)
                acc = a * acc + mm(p.astype(BF16), vb[kz, :, h * 128 : (h + 1) * 128])
                out.append((mn, l, acc))
            return tuple(out)

        start = (
            jnp.full((512, 1), NEG, F32),
            jnp.zeros((512, 1), F32),
            jnp.zeros((512, 128), F32),
        )
        done = lax.fori_loop(0, zq + 1, key_step, (start, start))
        for h in range(2):
            _, l, acc = done[h]
            out = (acc / l).astype(BF16)
            for j in range(4):
                att[zq, :, (4 * h + j) * 128 : (4 * h + j + 1) * 128] = out[j * 128 : (j + 1) * 128]
        return 0

    w_y[0].wait_recv()
    w_y[2].start()
    w_y[1].wait_recv()
    w_y[3].start()
    w_c[1].start()
    w_c[2].start()
    lax.fori_loop(0, 4, query_step, 0)
    w_y[2].wait_recv()
    w_y[3].wait_recv()
    w_c[3].start()
    for copy in w_c:
        copy.wait_recv()

    ids = lax.broadcasted_iota(jnp.int32, (TOK, EXPERTS), 1)
    hot = [ids == routes[:, k : k + 1] for k in range(2)]
    named = jnp.where(jnp.logical_or(hot[0], hot[1]), 1.0, 0.0).astype(BF16)
    earlier = jnp.where(
        lax.broadcasted_iota(jnp.int32, (TOK, TOK), 1) < lax.broadcasted_iota(jnp.int32, (TOK, TOK), 0),
        1.0,
        0.0,
    ).astype(BF16)
    before = mm(earlier, named)
    slot_ids = lax.broadcasted_iota(jnp.int32, (TOK, ROWS), 1)
    slot_hot = []
    for k in range(2):
        rank = jnp.sum(jnp.where(hot[k], before, 0.0), axis=1, keepdims=True).astype(jnp.int32)
        expert = routes[:, k : k + 1]
        slot = jnp.where(
            rank < MAIN, expert * MAIN + rank, EXPERTS * MAIN + expert * 2 + (rank - MAIN)
        )
        slot_hot.append(jnp.where(slot_ids == slot, 1.0, 0.0).astype(BF16))
    slot_any = slot_hot[0] + slot_hot[1]
    tpos = (z * 4 + x) * TOK + lax.broadcasted_iota(jnp.int32, (TOK, 1), 0)
    in_second = tpos >= bound
    own_len = jnp.where(in_second, second, bound).astype(F32)
    tall = lax.broadcasted_iota(jnp.int32, (TOK, REST), 0)
    wide = lax.broadcasted_iota(jnp.int32, (TOK, REST), 1)
    base = (wide // 2) * 16 + (wide % 2) * 8
    picks = [jnp.where(tall == base + kk, 1.0, 0.0).astype(BF16) for kk in range(6)]
    tall_t = lax.broadcasted_iota(jnp.int32, (REST, TOK), 0)
    wide_t = lax.broadcasted_iota(jnp.int32, (REST, TOK), 1)
    base_t = (tall_t // 2) * 16 + (tall_t % 2) * 8
    picks_t = [jnp.where(wide_t == base_t + kk, 1.0, 0.0).astype(BF16) for kk in range(6)]

    rsc = [
        [
            remote(part.at[c, i], rs.at[c, i], rs_s.at[c, i], rs_r.at[c, i], zp if i % 2 == 0 else zm)
            for i in range(6)
        ]
        for c in range(CHUNKS)
    ]

    def project(target, block):
        return mm(att[target], wb[block])

    def s1(c):
        for half in range(2):
            part[c, half] = project(z2, 2 * c + half).astype(BF16)
            rsc[c][half].start()

    def s2(c):
        part[c, 2] = project(z1, 2 * c + 1).astype(BF16)
        rsc[c][2].start()
        part[c, 3] = project(z3, 2 * c).astype(BF16)
        rsc[c][3].start()

    def s3(c):
        for half, target in ((0, z1), (1, z3)):
            through = project(target, 2 * c + half)
            rsc[c][half].wait_recv()
            part[c, 4 + half] = (through + rs[c, half].astype(F32)).astype(BF16)
            rsc[c][4 + half].start()

    state = {"square": jnp.zeros((TOK, 1), F32), "logits": jnp.zeros((TOK, EXPERTS), F32)}

    def s4(c):
        sums = []
        for half in range(2):
            span = slice((2 * c + half) * BLK, (2 * c + half + 1) * BLK)
            sums.append(res[:, span].astype(F32) + project(z, 2 * c + half))
        for i in (2, 3, 4, 5):
            rsc[c][i].wait_recv()
        for half, terms in ((0, (3, 4)), (1, (2, 5))):
            span = slice((2 * c + half) * BLK, (2 * c + half + 1) * BLK)
            h = sums[half] + rs[c, terms[0]].astype(F32) + rs[c, terms[1]].astype(F32)
            hid[:, span] = h
            state["square"] = state["square"] + jnp.sum(h * h, axis=1, keepdims=True)
            nrm[:, span] = (h * gain[:, span]).astype(BF16)
        span = slice(c * CW, (c + 1) * CW)
        r_all = router[:, span]
        r_hi = r_all.astype(BF16)
        r_rest = r_all - r_hi.astype(F32)
        r_mid = r_rest.astype(BF16)
        r_low = (r_rest - r_mid.astype(F32)).astype(BF16)
        rows_c = nrm[:, span]
        state["logits"] = (
            state["logits"] + rhs_t(rows_c, r_hi) + rhs_t(rows_c, r_mid) + rhs_t(rows_c, r_low)
        )

    own_slot = 2 * z
    my_rows = pl.ds(pl.multiple_of(e * MAIN, MAIN), MAIN)
    last = CHUNKS - 1
    wide_cols = lambda c: pl.ds(c * CW, CW + (EXT if c == last else 0))
    pack_cols = lambda c: pl.ds(c * 128, 256 if c == last else 128)
    y_copies, keep = [], []
    for c in range(CHUNKS):
        copies = []
        for d in range(1, 8):
            et = (e + d) % 8
            to = at(z, x, et)
            copies.append(
                remote(
                    stage.at[pl.ds(pl.multiple_of(et * MAIN, MAIN), MAIN), wide_cols(c)],
                    xb.at[own_slot, my_rows, wide_cols(c)],
                    y_s.at[c, 0, d - 1],
                    y_r.at[c, 0, d - 1],
                    to,
                )
            )
            copies.append(
                remote(
                    pack.at[et, :, pack_cols(c)],
                    unpack.at[e, :, pack_cols(c)],
                    y_s.at[c, 1, d - 1],
                    y_r.at[c, 1, d - 1],
                    to,
                )
            )
        y_copies.append(copies)
        keep.append(
            [
                pltpu.make_async_copy(
                    stage.at[my_rows, wide_cols(c)],
                    xb.at[own_slot, my_rows, wide_cols(c)],
                    lsem.at[8 + 2 * c],
                ),
                pltpu.make_async_copy(
                    pack.at[e, :, pack_cols(c)], unpack.at[e, :, pack_cols(c)], lsem.at[9 + 2 * c]
                ),
            ]
        )

    def scaled_ext():
        norm_scale = lax.rsqrt(state["square"] * (1.0 / D) + 1e-05)
        logits = state["logits"] * norm_scale
        picked = [jnp.sum(jnp.where(hot[k], logits, 0.0), axis=1, keepdims=True) for k in range(2)]
        gates = [
            1.0 / (1.0 + jnp.exp(picked[1] - picked[0])),
            1.0 / (1.0 + jnp.exp(picked[0] - picked[1])),
        ]
        lanes = lax.broadcasted_iota(jnp.int32, (TOK, EXT), 1)
        s_hi = norm_scale.astype(BF16).astype(F32)
        s_low = norm_scale - s_hi
        scales = jnp.where(lanes == 16, s_hi, jnp.where(lanes == 17, s_low, 0.0)).astype(BF16)
        ext = lhs_t(slot_any, scales)
        bucket = jnp.where(in_second, 8, 0) + e
        for k in range(2):
            weight = (gates[k] / own_len).astype(BF16).astype(F32)
            ext = ext + lhs_t(slot_hot[k], jnp.where(lanes == bucket, weight, 0.0).astype(BF16))
        stage[:, D:] = ext.astype(BF16)

    def send_y(c):
        span = slice(c * CW, (c + 1) * CW)
        stage[:, span] = lhs_t(slot_any, nrm[:, span]).astype(BF16)
        if c == last:
            scaled_ext()
        got = jnp.zeros((TOK, 128), F32)
        for kk in range(6):
            col = c * CW + kk * 128
            got = got + mm(picks[kk], stage[EXPERTS * MAIN :, col : col + 128])
        pack[:, :, c * 128 : (c + 1) * 128] = got.astype(BF16).reshape(EXPERTS, 16, 128)
        if c == last:
            got = mm(picks[0], stage[EXPERTS * MAIN :, D:])
            pack[:, :, (c + 1) * 128 : (c + 2) * 128] = got.astype(BF16).reshape(EXPERTS, 16, 128)
        for copy in y_copies[c] + keep[c]:
            copy.start()

    slot_of = lambda d: 2 * ((z + 4 - d) % 4)
    top, bottom = pl.ds(0, 128), pl.ds(128, ROWS - 128)

    def ring(c, side, s_sem, r_sem):
        cw = wide_cols(c)
        o, a, b = own_slot + side, slot_of(1) + side, slot_of(3) + side
        return [
            remote(xb.at[o, :, cw], xb.at[o, :, cw], s_sem(0), r_sem(0), zp),
            remote(xb.at[o, :, cw], xb.at[o, :, cw], s_sem(1), r_sem(1), zm),
            remote(xb.at[a, top, cw], xb.at[a, top, cw], s_sem(2), r_sem(2), zp),
            remote(xb.at[b, bottom, cw], xb.at[b, bottom, cw], s_sem(3), r_sem(3), zm),
        ]

    zc = [
        ring(c, 0, lambda i, c=c: z_s.at[c, i], lambda i, c=c: z_r.at[c, i]) for c in range(CHUNKS)
    ]
    zd = {
        c: ring(c, 1, lambda i, n=n: zd_s.at[n, i], lambda i, n=n: zd_r.at[n, i])
        for n, c in enumerate(X_FIRST)
    }
    xc = [
        [
            remote(
                xb.at[slot_of(d), :, wide_cols(c)],
                xb.at[slot_of(d) + 1, :, wide_cols(c)],
                x_s.at[c, d],
                x_r.at[c, d],
                partner_t,
            )
            for d in range(1 if c in X_FIRST else 4)
        ]
        for c in range(CHUNKS)
    ]

    def take_y(c):
        for copy in keep[c]:
            copy.wait()
        for copy in y_copies[c]:
            copy.wait_recv()
        flat = unpack[:, :, c * 128 : (c + 1) * 128].reshape(TOK, 128)
        for kk in range(6):
            col = c * CW + kk * 128
            xb[own_slot, EXPERTS * MAIN :, col : col + 128] = mm(picks_t[kk], flat).astype(BF16)
        if c == last:
            flat = unpack[:, :, (c + 1) * 128 : (c + 2) * 128].reshape(TOK, 128)
            xb[own_slot, EXPERTS * MAIN :, D:] = mm(picks_t[0], flat).astype(BF16)
        xc[c][0].start()
        zc[c][0].start()
        zc[c][1].start()

    def pass_x(c):
        xc[c][0].wait_recv()
        zd[c][0].start()
        zd[c][1].start()

    def pass_z(c):
        zc[c][0].wait_recv()
        zc[c][2].start()
        zc[c][1].wait_recv()
        zc[c][3].start()
        if c not in X_FIRST:
            xc[c][1].start()
            xc[c][3].start()

    def pass_zd(c):
        zd[c][0].wait_recv()
        zd[c][2].start()
        zd[c][1].wait_recv()
        zd[c][3].start()

    def pass_far(c):
        zc[c][2].wait_recv()
        zc[c][3].wait_recv()
        if c not in X_FIRST:
            xc[c][2].start()

    def experts(slot):
        def chunk_step(c, _):
            rows_x = xb[slot, :, :D]
            ext = xb[slot, :, D:]
            row_scale = ext[:, 16:17].astype(F32) + ext[:, 17:18].astype(F32)
            gate = mm(rows_x, wg[c]) * row_scale
            up = mm(rows_x, wu[c]) * row_scale
            act = (gate / (1.0 + jnp.exp(-gate)) * up).astype(BF16)
            hs[c] = hs[c] + lhs_t(ext, act)
            return 0

        lax.fori_loop(0, 4, chunk_step, 0)

    s1(0)
    s2(0)
    s1(1)
    s2(1)
    s3(0)
    s1(2)
    s2(2)
    s3(1)
    s4(0)
    send_y(0)
    s1(3)
    s2(3)
    s3(2)
    s4(1)
    send_y(1)
    take_y(0)
    s3(3)
    s4(2)
    send_y(2)
    take_y(1)
    s4(3)
    send_y(3)
    pass_z(0)
    take_y(2)
    pass_x(1)
    inv = 1.0 / own_len
    pool_out[...] = jnp.zeros_like(pool_out)
    pool_out[0:1] = jnp.sum(hid[...] * jnp.where(in_second, 0.0, inv), axis=0, keepdims=True)
    pool_out[1:2] = jnp.sum(hid[...] * jnp.where(in_second, inv, 0.0), axis=0, keepdims=True)
    hs[...] = jnp.zeros_like(hs)
    take_y(3)
    pass_z(1)
    pass_z(2)
    pass_zd(1)
    for copy in own_w:
        copy.wait()
    pass_z(3)
    for copy in far_w:
        copy.wait_recv()
    pass_far(0)
    experts(own_slot)
    pass_far(1)
    pass_far(2)
    for c in range(CHUNKS):
        if c not in X_FIRST:
            xc[c][0].wait_recv()
    experts(own_slot + 1)
    pass_far(3)
    experts(slot_of(1))
    experts(slot_of(3))
    experts(slot_of(2))
    for d in (1, 3, 2):
        for c in range(CHUNKS):
            if c not in X_FIRST:
                xc[c][d].wait_recv()
            elif d == 2:
                zd[c][2].wait_recv()
                zd[c][3].wait_recv()
        experts(slot_of(d) + 1)

    home = remote(hs.at[pl.ds(2, 2), pl.ds(0, 16)], hr, h_s, h_r, partner_w)
    home.start()
    home.wait_recv()
    for c in range(2):
        hs_out[:, c * 256 : (c + 1) * 256] = hs[c, 0:16] + hr[c]
    home.wait_send()
    started = [*q_z, *w_x, *w_y, *w_c, *far_w]
    for group in (*kv_z, *near, *far, *rsc, *y_copies, *zc, *zd.values(), *xc):
        started.extend(group)
    for copy in started:
        copy.wait_send()


def layer(lengths, q, k, v, op, res, gain, router_t, routes, w_gate, w_up):
    vmem = pl.BlockSpec(memory_space=pltpu.VMEM)
    hbm = pl.BlockSpec(memory_space=pl.ANY)
    dma = pltpu.SemaphoreType.DMA
    return pl.pallas_call(
        layer_kernel,
        out_shape=(
            jax.ShapeDtypeStruct((16, 512), F32),
            jax.ShapeDtypeStruct((8, D), F32),
        ),
        in_specs=[pl.BlockSpec(memory_space=pltpu.SMEM)] + [hbm] * 4 + [vmem] * 4 + [hbm, hbm],
        out_specs=(vmem, vmem),
        scratch_shapes=[
            pltpu.VMEM((4, TOK, 1024), BF16),
            pltpu.VMEM((4, 512, 256), BF16),
            pltpu.VMEM((4, 512, 256), BF16),
            pltpu.VMEM((4, TOK, 1024), BF16),
            pltpu.VMEM((8, 1024, BLK), BF16),
            pltpu.VMEM((CHUNKS, 6, TOK, BLK), BF16),
            pltpu.VMEM((CHUNKS, 6, TOK, BLK), BF16),
            pltpu.VMEM((TOK, D), F32),
            pltpu.VMEM((TOK, D), BF16),
            pltpu.VMEM((ROWS, WIDE), BF16),
            pltpu.VMEM((EXPERTS, 16, 128 * (CHUNKS + 1)), BF16),
            pltpu.VMEM((EXPERTS, 16, 128 * (CHUNKS + 1)), BF16),
            pltpu.VMEM((8, ROWS, WIDE), BF16),
            pltpu.VMEM((4, D, 256), BF16),
            pltpu.VMEM((4, D, 256), BF16),
            pltpu.VMEM((4, EXT, 256), F32),
            pltpu.VMEM((2, 16, 256), F32),
            dma((8 + 2 * CHUNKS,)),
            dma((3, 3)), dma((3, 3)),
            dma((6, 4)), dma((6, 4)),
            dma((11,)), dma((11,)),
            dma((CHUNKS, 6)), dma((CHUNKS, 6)),
            dma((4,)), dma((4,)),
            dma((CHUNKS, 2, 7)), dma((CHUNKS, 2, 7)),
            dma((CHUNKS, 4)), dma((CHUNKS, 4)),
            dma((max(1, len(X_FIRST)), 4)), dma((max(1, len(X_FIRST)), 4)),
            dma((CHUNKS, 4)), dma((CHUNKS, 4)),
            dma, dma,
        ],
        compiler_params=pltpu.CompilerParams(
            collective_id=0, has_side_effects=True, vmem_limit_bytes=VMEM_LIMIT
        ),
        cost_estimate=pl.CostEstimate(
            flops=36_000_000_000, bytes_accessed=24_000_000, transcendentals=8_000_000
        ),
        name="layer",
    )(lengths, q, k, v, op, res, gain, router_t, routes, w_gate, w_up)


def final_kernel(
    hs, pool, vec, head, wd, chosen, rejected,
    rew_out, loss_out, gh_out, wt_out,
    r_mine, r_exp, r_sum, r_seq, g_mine, g_exp, g_sum, g_seq,
    re_s, re_r, rq_s, rq_r, ge_s, ge_r, gq_s, gq_r,
):
    s = lax.axis_index("seq")
    e = lax.axis_index("exp")
    exp_peers = [(s, (e + d) % 8) for d in range(1, 8)]
    seq_peers = [((s + d) % 16, e) for d in range(1, 16)]
    greet(exp_peers + seq_peers)

    def all_sum(mine, got_exp, total, got_seq, es, er, qs, qr):
        copies = [
            remote(mine, got_exp.at[i], es.at[i], er.at[i], to) for i, to in enumerate(exp_peers)
        ]
        for copy in copies:
            copy.start()
        acc = mine[...]
        for i, copy in enumerate(copies):
            copy.wait_recv()
            acc = acc + got_exp[i]
        total[...] = acc
        more = [
            remote(total, got_seq.at[i], qs.at[i], qr.at[i], to) for i, to in enumerate(seq_peers)
        ]
        for copy in more:
            copy.start()
        for i, copy in enumerate(more):
            copy.wait_recv()
            acc = acc + got_seq[i]
        return acc, copies + more

    hsv = hs[...]
    part = jnp.sum(hsv * vec[...], axis=1, keepdims=True)
    own = jnp.sum(pool[...] * head[...], axis=1, keepdims=True)
    group = lax.broadcasted_iota(jnp.int32, (8, 128), 0)
    r_mine[0:8] = part[0:8] + jnp.where(group == e, own[0:1], 0.0)
    r_mine[8:16] = part[8:16] + jnp.where(group == e, own[1:2], 0.0)
    rewards, sent = all_sum(r_mine, r_exp, r_sum, r_seq, re_s, re_r, rq_s, rq_r)
    rew_out[...] = rewards

    r0, r1 = rewards[0:8], rewards[8:16]
    ch, rj = chosen[...], rejected[...]
    margin = jnp.where(ch == 0, r0, r1) - jnp.where(rj == 0, r0, r1)
    real = lax.broadcasted_iota(jnp.int32, (8, 128), 1) < 4
    loss = jnp.maximum(-margin, 0.0) + jnp.log1p(jnp.exp(-jnp.abs(margin)))
    loss = jnp.sum(jnp.where(real, loss, 0.0), axis=1, keepdims=True)
    loss = jnp.sum(loss, axis=0, keepdims=True) * (1.0 / 32.0)
    loss_out[...] = jnp.broadcast_to(loss, (8, 128))
    factor = jnp.where(real, -1.0 / (1.0 + jnp.exp(margin)) * (1.0 / 32.0), 0.0)
    up0 = jnp.where(ch == 0, factor, 0.0) - jnp.where(rj == 0, factor, 0.0)
    up1 = jnp.where(ch == 1, factor, 0.0) - jnp.where(rj == 1, factor, 0.0)
    rg0 = jnp.sum(up0, axis=1, keepdims=True)
    rg1 = jnp.sum(up1, axis=1, keepdims=True)
    weighted = jnp.sum(hsv[0:8] * rg0 + hsv[8:16] * rg1, axis=0, keepdims=True)
    wt_out[...] = jnp.broadcast_to(weighted, (8, 512))
    hi = weighted.astype(BF16).astype(F32)
    mid = (weighted - hi).astype(BF16).astype(F32)
    low = weighted - hi - mid
    line = lax.broadcasted_iota(jnp.int32, (16, 512), 0)
    three = jnp.where(line == 0, hi, jnp.where(line == 1, mid, jnp.where(line == 2, low, 0.0)))
    moved = jnp.sum(mm(three.astype(BF16), wd[...]), axis=0, keepdims=True)
    mine = lax.broadcasted_iota(jnp.int32, (8, 1), 0) == e
    own0 = jnp.sum(jnp.where(mine, rg0, 0.0), axis=0, keepdims=True)
    own1 = jnp.sum(jnp.where(mine, rg1, 0.0), axis=0, keepdims=True)
    grad = moved + own0 * pool[0:1] + own1 * pool[1:2]
    for i in range(24):
        g_mine[i : i + 1] = grad[:, i * 128 : (i + 1) * 128]
    total, more = all_sum(g_mine, g_exp, g_sum, g_seq, ge_s, ge_r, gq_s, gq_r)
    gh_out[...] = total
    for copy in sent + more:
        copy.wait_send()


def final(hs, pool, vec, head, wd, chosen, rejected):
    vmem = pl.BlockSpec(memory_space=pltpu.VMEM)
    dma = pltpu.SemaphoreType.DMA
    return pl.pallas_call(
        final_kernel,
        out_shape=(
            jax.ShapeDtypeStruct((16, 128), F32),
            jax.ShapeDtypeStruct((8, 128), F32),
            jax.ShapeDtypeStruct((24, 128), F32),
            jax.ShapeDtypeStruct((8, 512), F32),
        ),
        in_specs=[vmem] * 7,
        out_specs=(vmem,) * 4,
        scratch_shapes=[
            pltpu.VMEM((16, 128), F32), pltpu.VMEM((7, 16, 128), F32),
            pltpu.VMEM((16, 128), F32), pltpu.VMEM((15, 16, 128), F32),
            pltpu.VMEM((24, 128), F32), pltpu.VMEM((7, 24, 128), F32),
            pltpu.VMEM((24, 128), F32), pltpu.VMEM((15, 24, 128), F32),
            dma((7,)), dma((7,)), dma((15,)), dma((15,)),
            dma((7,)), dma((7,)), dma((15,)), dma((15,)),
        ],
        compiler_params=pltpu.CompilerParams(
            collective_id=1, has_side_effects=True, vmem_limit_bytes=VMEM_LIMIT
        ),
        name="final",
    )(hs, pool, vec, head, wd, chosen, rejected)


def per_device(
    query_states, key_states, value_states, residual, out_proj, norm_gain, router,
    w_gate, w_up, w_down, reward_head, lengths, routes, pair_list,
):
    vec = jnp.sum(w_down[0].astype(F32) * reward_head[None, :], axis=1)[None, :]
    hs, pool = layer(
        lengths, query_states[0], key_states[0], value_states[0], out_proj, residual[0],
        norm_gain[None, :], router.T, routes[0], w_gate[0], w_up[0],
    )
    pad = ((0, 0), (0, 124))
    rew, loss, gh, wt = final(
        hs, pool, vec, reward_head[None, :], w_down[0],
        jnp.pad(pair_list[:, :, 0], pad), jnp.pad(pair_list[:, :, 1], pad),
    )
    rewards = rew[:, 0].reshape(2, 8).T
    grad_down = (wt[0][:, None] * reward_head[None, :]).astype(BF16)[None]
    return rewards, loss[0, 0], gh.reshape(-1), grad_down


def solution(mesh):
    placed = (
        P("exp", "seq", None), P("exp", "seq", None), P("exp", "seq", None), P("exp", "seq", None),
        P("seq", None), P(), P(), P("exp", None, "seq"), P("exp", None, "seq"),
        P("exp", "seq", None), P(), P("exp", None), P("exp", "seq", None), P(),
    )
    return jax.shard_map(
        per_device,
        mesh=mesh,
        in_specs=placed,
        out_specs=(P(), P(), P(), P("exp", "seq", None)),
        check_vma=False,
    )
```

```python
import functools

import jax
import jax.numpy as jnp
from jax import lax
from jax.experimental import pallas as pl
from jax.experimental.pallas import tpu as pltpu
from jax.sharding import PartitionSpec as P

D = 3072
BLK = 384
CHUNKS = 4
CW = D // CHUNKS
X_FIRST = (1,)
EXT = 128
WIDE = D + EXT
Q_HEADS = 32
KV_HEADS = 8
HEAD_DIM = 128
SEQS = 2
TOK = 128
EXPERTS = 8
CAP = 34
ROWS = EXPERTS * CAP
MAIN = 32
REST = ROWS - EXPERTS * MAIN
NEG = -1e30
F32 = jnp.float32
BF16 = jnp.bfloat16
MESH = pl.DeviceIdType.MESH
VMEM_LIMIT = 60 * 1024 * 1024


def place():
    s = lax.axis_index("seq")
    e = lax.axis_index("exp")
    return s // 4, s % 4, e


def greet(devices):
    barrier = pltpu.get_barrier_semaphore()
    for device in devices:
        pl.semaphore_signal(barrier, inc=1, device_id=device, device_id_type=MESH)
    pl.semaphore_wait(barrier, len(devices))


def remote(src, dst, send, recv, device):
    return pltpu.make_async_remote_copy(
        src_ref=src, dst_ref=dst, send_sem=send, recv_sem=recv, device_id=device, device_id_type=MESH
    )


def lhs_t(a, b):
    return lax.dot_general(a, b, (((0,), (0,)), ((), ())), preferred_element_type=F32)


def rhs_t(a, b):
    return lax.dot_general(a, b, (((1,), (1,)), ((), ())), preferred_element_type=F32)


def mm(a, b):
    return jnp.dot(a, b, preferred_element_type=F32)


def three_rows(row, width):
    hi = row.astype(BF16).astype(F32)
    mid = (row - hi).astype(BF16).astype(F32)
    low = row - hi - mid
    line = lax.broadcasted_iota(jnp.int32, (16, width), 0)
    return jnp.where(line == 0, hi, jnp.where(line == 1, mid, jnp.where(line == 2, low, 0.0))).astype(BF16)


def layer_kernel(
    len_ref, q_ref, k_ref, v_ref, op_ref, res, gain, router, routes, wg_hbm, wu_hbm,
    wd_hbm, head, pairs,
    rew_out, loss_out, gh_out, wt_out,
    qb, kb, vb, att, wb, part, rs, hid, nrm, stage, pack, unpack, xb, wg, wu, hs, hr,
    lsem, zs, zr, xs, xr, o_s, o_r, rs_s, rs_r, w_s, w_r, y_s, y_r, z_s, z_r, zd_s, zd_r,
    x_s, x_r, h_s, h_r, wd, vec, vec_far, v_s, v_r, pool,
    r_mine, r_exp, r_sum, r_seq, g_mine, g_exp, g_sum, g_seq,
    re_s, re_r, rq_s, rq_r, ge_s, ge_r, gq_s, gq_r,
):
    z, x, e = place()
    core = e % 2
    at = lambda zz, xx, ee: (zz * 4 + xx, ee)
    z1, z2, z3 = (z + 1) % 4, (z + 2) % 4, (z + 3) % 4
    plus, across, minus = (x + 1) % 4, (x + 2) % 4, (x + 3) % 4
    swap, flip = x + 1 - 2 * (x % 2), 3 - x
    x_weight = swap * (1 - core) + flip * core
    x_token = flip * (1 - core) + swap * core
    zp, zm = at(z1, x, e), at(z3, x, e)
    xp, xm = at(z, plus, e), at(z, minus, e)
    partner_w, partner_t = at(z, x_weight, e), at(z, x_token, e)
    greet(
        [((z * 4 + x + d) % 16, e) for d in range(1, 16)]
        + [at(z, x, (e + d) % 8) for d in range(1, 8)]
    )

    wd_copy = pltpu.make_async_copy(wd_hbm, wd, lsem.at[8 + 2 * CHUNKS])
    mine = pl.ds(pl.multiple_of(x * TOK, TOK), TOK)
    cols_k = lambda zz: pl.ds(pl.multiple_of(zz * 256, 256), 256)
    cols_q = lambda zz: pl.ds(pl.multiple_of(zz * 1024, 1024), 1024)
    kv_z, q_z = [], []
    for d in (1, 2, 3):
        zt = (z + d) % 4
        to = at(zt, x, e)
        kv_z.append(
            (
                remote(k_ref.at[:, cols_k(zt)], kb.at[z, mine], zs.at[0, d - 1], zr.at[0, d - 1], to),
                remote(v_ref.at[:, cols_k(zt)], vb.at[z, mine], zs.at[1, d - 1], zr.at[1, d - 1], to),
            )
        )
        q_z.append(remote(q_ref.at[:, cols_q(zt)], qb.at[z], zs.at[2, d - 1], zr.at[2, d - 1], to))
    eighth = lambda ee: pl.ds(pl.multiple_of(ee * BLK, 128), BLK)
    row_of = lambda xx: pl.ds(pl.multiple_of(xx * 256, 256), 256)
    row_up = lambda xx: pl.ds(pl.multiple_of(xx * 256, 128), 128)
    row_low = lambda xx: pl.ds(pl.multiple_of(xx * 256 + 128, 128), 128)
    local = [
        pltpu.make_async_copy(k_ref.at[:, cols_k(z)], kb.at[z, mine], lsem.at[0]),
        pltpu.make_async_copy(v_ref.at[:, cols_k(z)], vb.at[z, mine], lsem.at[1]),
        pltpu.make_async_copy(q_ref.at[:, cols_q(z)], qb.at[z], lsem.at[2]),
        pltpu.make_async_copy(op_ref.at[:, eighth(e)], wb.at[row_of(x), eighth(e)], lsem.at[3]),
    ]
    def w_ring(cols, n):
        return [
            remote(op_ref.at[:, cols], wb.at[row_of(x), cols], o_s.at[n], o_r.at[n], xp),
            remote(op_ref.at[:, cols], wb.at[row_of(x), cols], o_s.at[n + 1], o_r.at[n + 1], xm),
            remote(
                wb.at[row_up(minus), cols], wb.at[row_up(minus), cols], o_s.at[n + 2], o_r.at[n + 2], xp
            ),
            remote(
                wb.at[row_low(plus), cols], wb.at[row_low(plus), cols], o_s.at[n + 3], o_r.at[n + 3], xm
            ),
        ]

    w_x = w_ring(eighth(e), 0)
    w_x[0].start()
    w_x[1].start()
    for d in (2, 1, 3):
        for copy in kv_z[d - 1]:
            copy.start()
    for copy in local + [wd_copy]:
        copy.start()
    for d in (2, 1, 3):
        q_z[d - 1].start()
    local[0].wait()
    local[1].wait()

    rows = lambda xx: pl.ds(pl.multiple_of(xx * TOK, TOK), TOK)
    near, far = [], []
    for d in (0, 1, 2, 3):
        zz = (z + 4 - d) % 4
        near.append(
            [
                remote(kb.at[zz, mine], kb.at[zz, mine], xs.at[0, d], xr.at[0, d], xp),
                remote(vb.at[zz, mine], vb.at[zz, mine], xs.at[1, d], xr.at[1, d], xp),
                remote(kb.at[zz, mine], kb.at[zz, mine], xs.at[2, d], xr.at[2, d], xm),
                remote(vb.at[zz, mine], vb.at[zz, mine], xs.at[3, d], xr.at[3, d], xm),
            ]
        )
        left, right = rows(minus), rows(plus)
        far.append(
            [
                remote(kb.at[zz, left], kb.at[zz, left], xs.at[4, d], xr.at[4, d], xp),
                remote(vb.at[zz, right], vb.at[zz, right], xs.at[5, d], xr.at[5, d], xm),
            ]
        )
    y_up, y_down = (e + 2) % 8, (e + 6) % 8
    other = e + 1 - 2 * core
    upper, lower = pl.ds(0, 512), pl.ds(512, 512)
    def over_y(part_rows, ee, n, to):
        ref = wb.at[part_rows, eighth(ee)]
        return remote(ref, ref, o_s.at[n], o_r.at[n], at(z, x, to))

    w_y = [
        over_y(upper, e, 8, y_up),
        over_y(lower, e, 9, y_down),
        over_y(lower, e, 10, y_up),
        over_y(upper, e, 11, y_down),
        over_y(upper, y_down, 12, y_up),
        over_y(lower, y_up, 13, y_down),
    ]
    w_c = [
        remote(wb.at[:, cols], wb.at[:, cols], o_s.at[14 + i], o_r.at[14 + i], at(z, x, other))
        for i, cols in enumerate(
            (eighth(e), eighth(y_down), eighth(y_up), eighth((e + 4) % 8))
        )
    ]
    w_x[0].wait_recv()
    w_x[2].start()
    w_x[1].wait_recv()
    w_x[3].start()
    for copy in near[0]:
        copy.start()
    local[3].wait()
    w_x[2].wait_recv()
    w_x[3].wait_recv()
    for copy in w_y[:4]:
        copy.start()
    w_c[0].start()
    order = (0, 1, 3, 2)
    for d in (1, 3, 2):
        kv_z[d - 1][0].wait_recv()
        kv_z[d - 1][1].wait_recv()
        for copy in near[d]:
            copy.start()
    wd_copy.wait()
    vec[...] = jnp.broadcast_to(
        jnp.sum(rhs_t(three_rows(head[...], D), wd[...]), axis=0, keepdims=True), (8, 512)
    )
    vec_copy = remote(vec, vec_far, v_s, v_r, partner_w)
    vec_copy.start()
    for d in order:
        near[d][0].wait_recv()
        far[d][0].start()
        near[d][3].wait_recv()
        far[d][1].start()
        if d == 1:
            w_y[0].wait_recv()
            w_y[4].start()
            w_y[1].wait_recv()
            w_y[5].start()
    for d in order:
        near[d][1].wait_recv()
        near[d][2].wait_recv()
        far[d][0].wait_recv()
        far[d][1].wait_recv()
    local[2].wait()
    for d in (1, 3, 2):
        q_z[d - 1].wait_recv()

    own_w, far_w = [], []
    for c in range(2):
        cols = pl.ds(c * 256, 256)
        for i, (hbm, buf) in enumerate(((wg_hbm, wg), (wu_hbm, wu))):
            own_w.append(pltpu.make_async_copy(hbm.at[:, cols], buf.at[c], lsem.at[4 + 2 * c + i]))
            far_w.append(
                remote(hbm.at[:, cols], buf.at[2 + c], w_s.at[2 * c + i], w_r.at[2 * c + i], partner_w)
            )
    for copy in far_w + own_w:
        copy.start()

    bound = len_ref[0, 0]
    second = len_ref[0, 1]
    scale = HEAD_DIM ** (-0.5) * 1.4426950408889634

    def query_step(zq, _):
        q_all = qb[zq]
        stacked = [
            jnp.concatenate(
                [q_all[:, (4 * h + j) * 128 : (4 * h + j + 1) * 128] for j in range(4)], axis=0
            )
            for h in range(2)
        ]
        qpos = (zq * 4 + x) * TOK + lax.broadcasted_iota(jnp.int32, (TOK, 512), 0)
        first = jnp.where(qpos >= bound, bound, 0)

        def key_step(kz, carry):
            kpos = kz * 512 + lax.broadcasted_iota(jnp.int32, (TOK, 512), 1)
            bias = jnp.where(jnp.logical_and(kpos <= qpos, kpos >= first), 0.0, NEG)
            out = []
            for h in range(2):
                m, l, acc = carry[h]
                sc = rhs_t(stacked[h], kb[kz, :, h * 128 : (h + 1) * 128])
                sc = (sc.reshape(4, TOK, 512) + bias[None]).reshape(512, 512)
                mn = jnp.maximum(m, jnp.max(sc, axis=1, keepdims=True))
                p = jnp.exp2((sc - mn) * scale)
                a = jnp.exp2((m - mn) * scale)
                l = a * l + jnp.sum(p, axis=1, keepdims=True)
                acc = a * acc + mm(p.astype(BF16), vb[kz, :, h * 128 : (h + 1) * 128])
                out.append((mn, l, acc))
            return tuple(out)

        start = (
            jnp.full((512, 1), NEG, F32),
            jnp.zeros((512, 1), F32),
            jnp.zeros((512, 128), F32),
        )
        done = lax.fori_loop(0, zq + 1, key_step, (start, start))
        for h in range(2):
            _, l, acc = done[h]
            out = (acc / l).astype(BF16)
            for j in range(4):
                att[zq, :, (4 * h + j) * 128 : (4 * h + j + 1) * 128] = out[j * 128 : (j + 1) * 128]
        return 0

    query_step(z2, 0)
    w_y[2].wait_recv()
    w_y[3].wait_recv()
    w_c[1].start()
    w_c[2].start()
    ids = lax.broadcasted_iota(jnp.int32, (TOK, EXPERTS), 1)
    hot = [ids == routes[:, k : k + 1] for k in range(2)]
    named = jnp.where(jnp.logical_or(hot[0], hot[1]), 1.0, 0.0).astype(BF16)
    earlier = jnp.where(
        lax.broadcasted_iota(jnp.int32, (TOK, TOK), 1) < lax.broadcasted_iota(jnp.int32, (TOK, TOK), 0),
        1.0,
        0.0,
    ).astype(BF16)
    before = mm(earlier, named)
    slot_ids = lax.broadcasted_iota(jnp.int32, (TOK, ROWS), 1)
    slot_hot = []
    for k in range(2):
        rank = jnp.sum(jnp.where(hot[k], before, 0.0), axis=1, keepdims=True).astype(jnp.int32)
        expert = routes[:, k : k + 1]
        slot = jnp.where(
            rank < MAIN, expert * MAIN + rank, EXPERTS * MAIN + expert * 2 + (rank - MAIN)
        )
        slot_hot.append(jnp.where(slot_ids == slot, 1.0, 0.0).astype(BF16))
    slot_any = slot_hot[0] + slot_hot[1]
    tpos = (z * 4 + x) * TOK + lax.broadcasted_iota(jnp.int32, (TOK, 1), 0)
    in_second = tpos >= bound
    own_len = jnp.where(in_second, second, bound).astype(F32)
    tall = lax.broadcasted_iota(jnp.int32, (TOK, REST), 0)
    wide = lax.broadcasted_iota(jnp.int32, (TOK, REST), 1)
    base = (wide // 2) * 16 + (wide % 2) * 8
    picks = [jnp.where(tall == base + kk, 1.0, 0.0).astype(BF16) for kk in range(6)]
    tall_t = lax.broadcasted_iota(jnp.int32, (REST, TOK), 0)
    wide_t = lax.broadcasted_iota(jnp.int32, (REST, TOK), 1)
    base_t = (tall_t // 2) * 16 + (tall_t % 2) * 8
    picks_t = [jnp.where(wide_t == base_t + kk, 1.0, 0.0).astype(BF16) for kk in range(6)]

    rsc = [
        [
            remote(part.at[c, i], rs.at[c, i], rs_s.at[c, i], rs_r.at[c, i], zp if i % 2 == 0 else zm)
            for i in range(6)
        ]
        for c in range(CHUNKS)
    ]

    def project(target, block):
        return mm(att[target], wb[:, block * BLK : (block + 1) * BLK])

    def s1(c):
        for half in range(2):
            part[c, half] = project(z2, 2 * c + half).astype(BF16)
            rsc[c][half].start()

    def s2(c):
        part[c, 2] = project(z1, 2 * c + 1).astype(BF16)
        rsc[c][2].start()
        part[c, 3] = project(z3, 2 * c).astype(BF16)
        rsc[c][3].start()

    def s3(c):
        for half, target in ((0, z1), (1, z3)):
            through = project(target, 2 * c + half)
            rsc[c][half].wait_recv()
            part[c, 4 + half] = (through + rs[c, half].astype(F32)).astype(BF16)
            rsc[c][4 + half].start()

    state = {"square": jnp.zeros((TOK, 1), F32), "logits": jnp.zeros((TOK, EXPERTS), F32)}

    def s4(c):
        sums = []
        for half in range(2):
            span = slice((2 * c + half) * BLK, (2 * c + half + 1) * BLK)
            sums.append(res[:, span].astype(F32) + project(z, 2 * c + half))
        for i in (2, 3, 4, 5):
            rsc[c][i].wait_recv()
        for half, terms in ((0, (3, 4)), (1, (2, 5))):
            span = slice((2 * c + half) * BLK, (2 * c + half + 1) * BLK)
            h = sums[half] + rs[c, terms[0]].astype(F32) + rs[c, terms[1]].astype(F32)
            hid[:, span] = h
            state["square"] = state["square"] + jnp.sum(h * h, axis=1, keepdims=True)
            nrm[:, span] = (h * gain[:, span]).astype(BF16)
        span = slice(c * CW, (c + 1) * CW)
        r_all = router[:, span]
        r_hi = r_all.astype(BF16)
        r_rest = r_all - r_hi.astype(F32)
        r_mid = r_rest.astype(BF16)
        r_low = (r_rest - r_mid.astype(F32)).astype(BF16)
        rows_c = nrm[:, span]
        state["logits"] = (
            state["logits"] + rhs_t(rows_c, r_hi) + rhs_t(rows_c, r_mid) + rhs_t(rows_c, r_low)
        )

    own_slot = 2 * z
    my_rows = pl.ds(pl.multiple_of(e * MAIN, MAIN), MAIN)
    last = CHUNKS - 1
    wide_cols = lambda c: pl.ds(c * CW, CW + (EXT if c == last else 0))
    pack_cols = lambda c: pl.ds(c * 128, 256 if c == last else 128)
    y_copies, keep = [], []
    for c in range(CHUNKS):
        copies = []
        for d in range(1, 8):
            et = (e + d) % 8
            to = at(z, x, et)
            copies.append(
                remote(
                    stage.at[pl.ds(pl.multiple_of(et * MAIN, MAIN), MAIN), wide_cols(c)],
                    xb.at[own_slot, my_rows, wide_cols(c)],
                    y_s.at[c, 0, d - 1],
                    y_r.at[c, 0, d - 1],
                    to,
                )
            )
            copies.append(
                remote(
                    pack.at[et, :, pack_cols(c)],
                    unpack.at[e, :, pack_cols(c)],
                    y_s.at[c, 1, d - 1],
                    y_r.at[c, 1, d - 1],
                    to,
                )
            )
        y_copies.append(copies)
        keep.append(
            [
                pltpu.make_async_copy(
                    stage.at[my_rows, wide_cols(c)],
                    xb.at[own_slot, my_rows, wide_cols(c)],
                    lsem.at[8 + 2 * c],
                ),
                pltpu.make_async_copy(
                    pack.at[e, :, pack_cols(c)], unpack.at[e, :, pack_cols(c)], lsem.at[9 + 2 * c]
                ),
            ]
        )

    def scaled_ext():
        norm_scale = lax.rsqrt(state["square"] * (1.0 / D) + 1e-05)
        logits = state["logits"] * norm_scale
        picked = [jnp.sum(jnp.where(hot[k], logits, 0.0), axis=1, keepdims=True) for k in range(2)]
        gates = [
            1.0 / (1.0 + jnp.exp(picked[1] - picked[0])),
            1.0 / (1.0 + jnp.exp(picked[0] - picked[1])),
        ]
        lanes = lax.broadcasted_iota(jnp.int32, (TOK, EXT), 1)
        s_hi = norm_scale.astype(BF16).astype(F32)
        s_low = norm_scale - s_hi
        scales = jnp.where(lanes == 16, s_hi, jnp.where(lanes == 17, s_low, 0.0)).astype(BF16)
        ext = lhs_t(slot_any, scales)
        bucket = jnp.where(in_second, 8, 0) + e
        for k in range(2):
            weight = (gates[k] / own_len).astype(BF16).astype(F32)
            ext = ext + lhs_t(slot_hot[k], jnp.where(lanes == bucket, weight, 0.0).astype(BF16))
        stage[:, D:] = ext.astype(BF16)

    def send_y(c):
        span = slice(c * CW, (c + 1) * CW)
        stage[:, span] = lhs_t(slot_any, nrm[:, span]).astype(BF16)
        if c == last:
            scaled_ext()
        got = jnp.zeros((TOK, 128), F32)
        for kk in range(6):
            col = c * CW + kk * 128
            got = got + mm(picks[kk], stage[EXPERTS * MAIN :, col : col + 128])
        pack[:, :, c * 128 : (c + 1) * 128] = got.astype(BF16).reshape(EXPERTS, 16, 128)
        if c == last:
            got = mm(picks[0], stage[EXPERTS * MAIN :, D:])
            pack[:, :, (c + 1) * 128 : (c + 2) * 128] = got.astype(BF16).reshape(EXPERTS, 16, 128)
        for copy in y_copies[c] + keep[c]:
            copy.start()

    slot_of = lambda d: 2 * ((z + 4 - d) % 4)
    top, bottom = pl.ds(0, 128), pl.ds(128, ROWS - 128)

    def ring(c, side, s_sem, r_sem):
        cw = wide_cols(c)
        o, a, b = own_slot + side, slot_of(1) + side, slot_of(3) + side
        return [
            remote(xb.at[o, :, cw], xb.at[o, :, cw], s_sem(0), r_sem(0), zp),
            remote(xb.at[o, :, cw], xb.at[o, :, cw], s_sem(1), r_sem(1), zm),
            remote(xb.at[a, top, cw], xb.at[a, top, cw], s_sem(2), r_sem(2), zp),
            remote(xb.at[b, bottom, cw], xb.at[b, bottom, cw], s_sem(3), r_sem(3), zm),
        ]

    zc = [
        ring(c, 0, lambda i, c=c: z_s.at[c, i], lambda i, c=c: z_r.at[c, i]) for c in range(CHUNKS)
    ]
    zd = {
        c: ring(c, 1, lambda i, n=n: zd_s.at[n, i], lambda i, n=n: zd_r.at[n, i])
        for n, c in enumerate(X_FIRST)
    }
    xc = [
        [
            remote(
                xb.at[slot_of(d), :, wide_cols(c)],
                xb.at[slot_of(d) + 1, :, wide_cols(c)],
                x_s.at[c, d],
                x_r.at[c, d],
                partner_t,
            )
            for d in range(1 if c in X_FIRST else 4)
        ]
        for c in range(CHUNKS)
    ]

    def take_y(c):
        for copy in keep[c]:
            copy.wait()
        for copy in y_copies[c]:
            copy.wait_recv()
        flat = unpack[:, :, c * 128 : (c + 1) * 128].reshape(TOK, 128)
        for kk in range(6):
            col = c * CW + kk * 128
            xb[own_slot, EXPERTS * MAIN :, col : col + 128] = mm(picks_t[kk], flat).astype(BF16)
        if c == last:
            flat = unpack[:, :, (c + 1) * 128 : (c + 2) * 128].reshape(TOK, 128)
            xb[own_slot, EXPERTS * MAIN :, D:] = mm(picks_t[0], flat).astype(BF16)
        xc[c][0].start()
        zc[c][0].start()
        zc[c][1].start()

    def pass_x(c):
        xc[c][0].wait_recv()
        zd[c][0].start()
        zd[c][1].start()

    def pass_z(c):
        zc[c][0].wait_recv()
        zc[c][2].start()
        zc[c][1].wait_recv()
        zc[c][3].start()
        if c not in X_FIRST:
            xc[c][1].start()
            xc[c][3].start()

    def pass_zd(c):
        zd[c][0].wait_recv()
        zd[c][2].start()
        zd[c][1].wait_recv()
        zd[c][3].start()

    def pass_far(c):
        zc[c][2].wait_recv()
        zc[c][3].wait_recv()
        if c not in X_FIRST:
            xc[c][2].start()

    def experts(slot, low, high):
        def chunk_step(c, _):
            rows_x = xb[slot, :, :D]
            ext = xb[slot, :, D:]
            row_scale = ext[:, 16:17].astype(F32) + ext[:, 17:18].astype(F32)
            gate = mm(rows_x, wg[c]) * row_scale
            up = mm(rows_x, wu[c]) * row_scale
            act = (gate / (1.0 + jnp.exp(-gate)) * up).astype(BF16)
            hs[c] = hs[c] + lhs_t(ext, act)
            return 0

        lax.fori_loop(low, high, chunk_step, 0)

    w_y[4].wait_recv()
    w_y[5].wait_recv()
    w_c[3].start()
    for copy in w_c:
        copy.wait_recv()
    for c in range(CHUNKS):
        s1(c)
    lax.fori_loop(0, 2, lambda i, _: query_step((z1 + 2 * i) % 4, _), 0)
    s2(0)
    s3(0)
    s2(1)
    s3(1)
    query_step(z, 0)
    s2(2)
    s3(2)
    s4(0)
    send_y(0)
    s2(3)
    s4(1)
    send_y(1)
    take_y(0)
    s3(3)
    s4(2)
    send_y(2)
    take_y(1)
    s4(3)
    send_y(3)
    pass_z(0)
    take_y(2)
    pass_x(1)
    inv = 1.0 / own_len
    pool[...] = jnp.zeros_like(pool)
    pool[0:1] = jnp.sum(hid[...] * jnp.where(in_second, 0.0, inv), axis=0, keepdims=True)
    pool[1:2] = jnp.sum(hid[...] * jnp.where(in_second, inv, 0.0), axis=0, keepdims=True)
    hs[...] = jnp.zeros_like(hs)
    take_y(3)
    pass_z(1)
    for copy in own_w:
        copy.wait()
    experts(own_slot, 0, 2)
    pass_z(2)
    pass_zd(1)
    for c in range(CHUNKS):
        if c not in X_FIRST:
            xc[c][0].wait_recv()
    experts(own_slot + 1, 0, 2)
    pass_z(3)
    for copy in far_w:
        copy.wait_recv()
    pass_far(0)
    experts(own_slot, 2, 4)
    experts(own_slot + 1, 2, 4)
    pass_far(1)
    experts(slot_of(1), 0, 4)
    pass_far(2)
    pass_far(3)
    experts(slot_of(3), 0, 4)
    for d in (1, 3, 2):
        if d == 2:
            experts(slot_of(2), 0, 4)
        for c in range(CHUNKS):
            if c not in X_FIRST:
                xc[c][d].wait_recv()
            elif d == 2:
                zd[c][2].wait_recv()
                zd[c][3].wait_recv()
        experts(slot_of(d) + 1, 0, 4)

    home = remote(hs.at[pl.ds(2, 2), pl.ds(0, 16)], hr, h_s, h_r, partner_w)
    home.start()
    vec_copy.wait_recv()
    s = z * 4 + x
    exp_peers = [(s, (e + d) % 8) for d in range(1, 8)]
    seq_peers = [((s + d) % 16, e) for d in range(1, 16)]

    def all_sum(mine, got_exp, total, got_seq, es, er, qs, qr):
        copies = [
            remote(mine, got_exp.at[i], es.at[i], er.at[i], to) for i, to in enumerate(exp_peers)
        ]
        for copy in copies:
            copy.start()
        acc = mine[...]
        for i, copy in enumerate(copies):
            copy.wait_recv()
            acc = acc + got_exp[i]
        total[...] = acc
        more = [
            remote(total, got_seq.at[i], qs.at[i], qr.at[i], to) for i, to in enumerate(seq_peers)
        ]
        for copy in more:
            copy.start()
        for i, copy in enumerate(more):
            copy.wait_recv()
            acc = acc + got_seq[i]
        return acc, copies + more

    part_r = jnp.zeros((16, 1), F32)
    for c in range(2):
        span = slice(c * 256, (c + 1) * 256)
        part_r = part_r + jnp.sum(
            hs[c, 0:16] * vec[0:1, span] + hs[2 + c, 0:16] * vec_far[0:1, span], axis=1, keepdims=True
        )
    own = jnp.sum(pool[...] * head[...], axis=1, keepdims=True)
    group = lax.broadcasted_iota(jnp.int32, (8, 128), 0)
    r_mine[0:8] = part_r[0:8] + jnp.where(group == e, own[0:1], 0.0)
    r_mine[8:16] = part_r[8:16] + jnp.where(group == e, own[1:2], 0.0)
    rewards, sent = all_sum(r_mine, r_exp, r_sum, r_seq, re_s, re_r, rq_s, rq_r)

    home.wait_recv()
    hsv = jnp.concatenate([hs[c, 0:16] + hr[c] for c in range(2)], axis=1)
    r0, r1 = rewards[0:8], rewards[8:16]
    lane = lax.broadcasted_iota(jnp.int32, (8, 128), 1)
    rew_out[...] = jnp.where(lane == 0, r0, r1)[:, :2]
    named_pair = pairs[...]
    value = jnp.where(named_pair == 0, r0, r1)
    margin = value - pltpu.roll(value, 127, 1)
    real = jnp.logical_and(lane % 2 == 0, lane < 8)
    loss = jnp.maximum(-margin, 0.0) + jnp.log1p(jnp.exp(-jnp.abs(margin)))
    loss = jnp.sum(jnp.where(real, loss, 0.0), axis=1, keepdims=True)
    loss_out[...] = jnp.sum(loss, axis=0, keepdims=True) * (1.0 / 32.0)
    factor = jnp.where(real, -1.0 / (1.0 + jnp.exp(margin)) * (1.0 / 32.0), 0.0)
    factor = factor - pltpu.roll(factor, 1, 1)
    rg0 = jnp.sum(jnp.where(named_pair == 0, factor, 0.0), axis=1, keepdims=True)
    rg1 = jnp.sum(jnp.where(named_pair == 1, factor, 0.0), axis=1, keepdims=True)
    weighted = jnp.sum(hsv[0:8] * rg0 + hsv[8:16] * rg1, axis=0, keepdims=True)
    wt_out[...] = weighted
    moved = jnp.sum(mm(three_rows(weighted, 512), wd[...]), axis=0, keepdims=True)
    me_row = lax.broadcasted_iota(jnp.int32, (8, 1), 0) == e
    own0 = jnp.sum(jnp.where(me_row, rg0, 0.0), axis=0, keepdims=True)
    own1 = jnp.sum(jnp.where(me_row, rg1, 0.0), axis=0, keepdims=True)
    grad = moved + own0 * pool[0:1] + own1 * pool[1:2]
    for i in range(24):
        g_mine[i : i + 1] = grad[:, i * 128 : (i + 1) * 128]
    gh_out[...], more = all_sum(g_mine, g_exp, g_sum, g_seq, ge_s, ge_r, gq_s, gq_r)

    started = [home, vec_copy, *sent, *more, *q_z, *w_x, *w_y, *w_c, *far_w]
    for group in (*kv_z, *near, *far, *rsc, *y_copies, *zc, *zd.values(), *xc):
        started.extend(group)
    for copy in started:
        copy.wait_send()


def layer(lengths, q, k, v, op, res, gain, router_t, routes, w_gate, w_up, w_down, head, pairs):
    vmem = pl.BlockSpec(memory_space=pltpu.VMEM)
    hbm = pl.BlockSpec(memory_space=pl.ANY)
    dma = pltpu.SemaphoreType.DMA
    return pl.pallas_call(
        layer_kernel,
        out_shape=(
            jax.ShapeDtypeStruct((EXPERTS, SEQS), F32),
            jax.ShapeDtypeStruct((1, 1), F32),
            jax.ShapeDtypeStruct((24, 128), F32),
            jax.ShapeDtypeStruct((1, 512), F32),
        ),
        in_specs=[pl.BlockSpec(memory_space=pltpu.SMEM)] + [hbm] * 4 + [vmem] * 4 + [hbm] * 3 + [vmem] * 2,
        out_specs=(vmem,) * 4,
        scratch_shapes=[
            pltpu.VMEM((4, TOK, 1024), BF16),
            pltpu.VMEM((4, 512, 256), BF16),
            pltpu.VMEM((4, 512, 256), BF16),
            pltpu.VMEM((4, TOK, 1024), BF16),
            pltpu.VMEM((1024, D), BF16),
            pltpu.VMEM((CHUNKS, 6, TOK, BLK), BF16),
            pltpu.VMEM((CHUNKS, 6, TOK, BLK), BF16),
            pltpu.VMEM((TOK, D), F32),
            pltpu.VMEM((TOK, D), BF16),
            pltpu.VMEM((ROWS, WIDE), BF16),
            pltpu.VMEM((EXPERTS, 16, 128 * (CHUNKS + 1)), BF16),
            pltpu.VMEM((EXPERTS, 16, 128 * (CHUNKS + 1)), BF16),
            pltpu.VMEM((8, ROWS, WIDE), BF16),
            pltpu.VMEM((4, D, 256), BF16),
            pltpu.VMEM((4, D, 256), BF16),
            pltpu.VMEM((4, EXT, 256), F32),
            pltpu.VMEM((2, 16, 256), F32),
            dma((10 + 2 * CHUNKS,)),
            dma((3, 3)), dma((3, 3)),
            dma((6, 4)), dma((6, 4)),
            dma((19,)), dma((19,)),
            dma((CHUNKS, 6)), dma((CHUNKS, 6)),
            dma((4,)), dma((4,)),
            dma((CHUNKS, 2, 7)), dma((CHUNKS, 2, 7)),
            dma((CHUNKS, 4)), dma((CHUNKS, 4)),
            dma((max(1, len(X_FIRST)), 4)), dma((max(1, len(X_FIRST)), 4)),
            dma((CHUNKS, 4)), dma((CHUNKS, 4)),
            dma, dma,
            pltpu.VMEM((512, D), BF16), pltpu.VMEM((8, 512), F32), pltpu.VMEM((8, 512), F32), dma, dma, pltpu.VMEM((8, D), F32),
            pltpu.VMEM((16, 128), F32), pltpu.VMEM((7, 16, 128), F32),
            pltpu.VMEM((16, 128), F32), pltpu.VMEM((15, 16, 128), F32),
            pltpu.VMEM((24, 128), F32), pltpu.VMEM((7, 24, 128), F32),
            pltpu.VMEM((24, 128), F32), pltpu.VMEM((15, 24, 128), F32),
            dma((7,)), dma((7,)), dma((15,)), dma((15,)),
            dma((7,)), dma((7,)), dma((15,)), dma((15,)),
        ],
        compiler_params=pltpu.CompilerParams(
            collective_id=0, has_side_effects=True, vmem_limit_bytes=VMEM_LIMIT
        ),
        cost_estimate=pl.CostEstimate(
            flops=36_000_000_000, bytes_accessed=24_000_000, transcendentals=8_000_000
        ),
        name="layer",
    )(lengths, q, k, v, op, res, gain, router_t, routes, w_gate, w_up, w_down, head, pairs)


def per_device(
    query_states, key_states, value_states, residual, out_proj, norm_gain, router,
    w_gate, w_up, w_down, reward_head, lengths, routes, pair_list,
):
    pairs = jnp.pad(pair_list.reshape(8, 8), ((0, 0), (0, 120)))
    rewards, loss, gh, wt = layer(
        lengths, query_states[0], key_states[0], value_states[0], out_proj, residual[0],
        norm_gain[None, :], router.T, routes[0], w_gate[0], w_up[0], w_down[0],
        reward_head[None, :], pairs,
    )
    grad_down = (wt[0][:, None] * reward_head[None, :]).astype(BF16)[None]
    return rewards, loss.reshape(()), gh.reshape(-1), grad_down


def solution(mesh):
    placed = (
        P("exp", "seq", None), P("exp", "seq", None), P("exp", "seq", None), P("exp", "seq", None),
        P("seq", None), P(), P(), P("exp", None, "seq"), P("exp", None, "seq"),
        P("exp", "seq", None), P(), P("exp", None), P("exp", "seq", None), P(),
    )
    return jax.shard_map(
        per_device,
        mesh=mesh,
        in_specs=placed,
        out_specs=(P(), P(), P(), P("exp", "seq", None)),
        check_vma=False,
    )
```

```python
import functools

import jax
import jax.numpy as jnp
from jax import lax
from jax.experimental import pallas as pl
from jax.experimental.pallas import tpu as pltpu
from jax.sharding import PartitionSpec as P

D = 3072
BLK = 384
CHUNKS = 4
CW = D // CHUNKS
X_FIRST = (1,)
EXT = 128
WIDE = D + EXT
Q_HEADS = 32
KV_HEADS = 8
HEAD_DIM = 128
SEQS = 2
TOK = 128
EXPERTS = 8
CAP = 34
ROWS = EXPERTS * CAP
MAIN = 32
REST = ROWS - EXPERTS * MAIN
NEG = -1e30
F32 = jnp.float32
BF16 = jnp.bfloat16
MESH = pl.DeviceIdType.MESH
VMEM_LIMIT = 60 * 1024 * 1024


def place():
    s = lax.axis_index("seq")
    e = lax.axis_index("exp")
    return s // 4, s % 4, e


def greet(devices):
    barrier = pltpu.get_barrier_semaphore()
    for device in devices:
        pl.semaphore_signal(barrier, inc=1, device_id=device, device_id_type=MESH)
    pl.semaphore_wait(barrier, len(devices))


def remote(src, dst, send, recv, device):
    return pltpu.make_async_remote_copy(
        src_ref=src, dst_ref=dst, send_sem=send, recv_sem=recv, device_id=device, device_id_type=MESH
    )


def lhs_t(a, b):
    return lax.dot_general(a, b, (((0,), (0,)), ((), ())), preferred_element_type=F32)


def rhs_t(a, b):
    return lax.dot_general(a, b, (((1,), (1,)), ((), ())), preferred_element_type=F32)


def mm(a, b):
    return jnp.dot(a, b, preferred_element_type=F32)


def three_rows(row, width):
    hi = row.astype(BF16).astype(F32)
    mid = (row - hi).astype(BF16).astype(F32)
    low = row - hi - mid
    line = lax.broadcasted_iota(jnp.int32, (16, width), 0)
    return jnp.where(line == 0, hi, jnp.where(line == 1, mid, jnp.where(line == 2, low, 0.0))).astype(BF16)


def layer_kernel(
    len_ref, q_ref, k_ref, v_ref, op_ref, res, gain, router, routes, wg_hbm, wu_hbm,
    wd_hbm, head, pairs,
    rew_out, loss_out, gh_out, wt_out,
    qb, kb, vb, att, wb, part, rs, hid, nrm, stage, pack, unpack, xb, wg, wu, hs, hr,
    lsem, zs, zr, xs, xr, o_s, o_r, rs_s, rs_r, w_s, w_r, y_s, y_r, z_s, z_r, zd_s, zd_r,
    x_s, x_r, h_s, h_r, wd, vec, vec_far, v_s, v_r, kept, pool,
    r_mine, r_exp, r_sum, r_seq, g_mine, g_exp, g_sum, g_seq,
    re_s, re_r, rq_s, rq_r, ge_s, ge_r, gq_s, gq_r,
):
    z, x, e = place()
    core = e % 2
    at = lambda zz, xx, ee: (zz * 4 + xx, ee)
    z1, z2, z3 = (z + 1) % 4, (z + 2) % 4, (z + 3) % 4
    plus, across, minus = (x + 1) % 4, (x + 2) % 4, (x + 3) % 4
    swap, flip = x + 1 - 2 * (x % 2), 3 - x
    x_weight = swap * (1 - core) + flip * core
    x_token = flip * (1 - core) + swap * core
    zp, zm = at(z1, x, e), at(z3, x, e)
    xp, xm = at(z, plus, e), at(z, minus, e)
    partner_w, partner_t = at(z, x_weight, e), at(z, x_token, e)
    greet(
        [((z * 4 + x + d) % 16, e) for d in range(1, 16)]
        + [at(z, x, (e + d) % 8) for d in range(1, 8)]
    )

    wd_copy = pltpu.make_async_copy(wd_hbm, wd, lsem.at[8 + 2 * CHUNKS])
    mine = pl.ds(pl.multiple_of(x * TOK, TOK), TOK)
    cols_k = lambda zz: pl.ds(pl.multiple_of(zz * 256, 256), 256)
    cols_q = lambda zz: pl.ds(pl.multiple_of(zz * 1024, 1024), 1024)
    kv_z, q_z = [], []
    for d in (1, 2, 3):
        zt = (z + d) % 4
        to = at(zt, x, e)
        kv_z.append(
            (
                remote(k_ref.at[:, cols_k(zt)], kb.at[z, mine], zs.at[0, d - 1], zr.at[0, d - 1], to),
                remote(v_ref.at[:, cols_k(zt)], vb.at[z, mine], zs.at[1, d - 1], zr.at[1, d - 1], to),
            )
        )
        q_z.append(remote(q_ref.at[:, cols_q(zt)], qb.at[z], zs.at[2, d - 1], zr.at[2, d - 1], to))
    eighth = lambda ee: pl.ds(pl.multiple_of(ee * BLK, 128), BLK)
    row_of = lambda xx: pl.ds(pl.multiple_of(xx * 256, 256), 256)
    row_up = lambda xx: pl.ds(pl.multiple_of(xx * 256, 128), 128)
    row_low = lambda xx: pl.ds(pl.multiple_of(xx * 256 + 128, 128), 128)
    local = [
        pltpu.make_async_copy(k_ref.at[:, cols_k(z)], kb.at[z, mine], lsem.at[0]),
        pltpu.make_async_copy(v_ref.at[:, cols_k(z)], vb.at[z, mine], lsem.at[1]),
        pltpu.make_async_copy(q_ref.at[:, cols_q(z)], qb.at[z], lsem.at[2]),
        pltpu.make_async_copy(op_ref.at[:, eighth(e)], wb.at[row_of(x), eighth(e)], lsem.at[3]),
    ]
    def w_ring(cols, n):
        return [
            remote(op_ref.at[:, cols], wb.at[row_of(x), cols], o_s.at[n], o_r.at[n], xp),
            remote(op_ref.at[:, cols], wb.at[row_of(x), cols], o_s.at[n + 1], o_r.at[n + 1], xm),
            remote(
                wb.at[row_up(minus), cols], wb.at[row_up(minus), cols], o_s.at[n + 2], o_r.at[n + 2], xp
            ),
            remote(
                wb.at[row_low(plus), cols], wb.at[row_low(plus), cols], o_s.at[n + 3], o_r.at[n + 3], xm
            ),
        ]

    w_x = w_ring(eighth(e), 0)
    w_x[0].start()
    w_x[1].start()
    for d in (2, 1, 3):
        for copy in kv_z[d - 1]:
            copy.start()
    for copy in local + [wd_copy]:
        copy.start()
    for d in (2, 1, 3):
        q_z[d - 1].start()
    local[0].wait()
    local[1].wait()

    rows = lambda xx: pl.ds(pl.multiple_of(xx * TOK, TOK), TOK)
    near, far = [], []
    for d in (0, 1, 2, 3):
        zz = (z + 4 - d) % 4
        near.append(
            [
                remote(kb.at[zz, mine], kb.at[zz, mine], xs.at[0, d], xr.at[0, d], xp),
                remote(vb.at[zz, mine], vb.at[zz, mine], xs.at[1, d], xr.at[1, d], xp),
                remote(kb.at[zz, mine], kb.at[zz, mine], xs.at[2, d], xr.at[2, d], xm),
                remote(vb.at[zz, mine], vb.at[zz, mine], xs.at[3, d], xr.at[3, d], xm),
            ]
        )
        left, right = rows(minus), rows(plus)
        far.append(
            [
                remote(kb.at[zz, left], kb.at[zz, left], xs.at[4, d], xr.at[4, d], xp),
                remote(vb.at[zz, right], vb.at[zz, right], xs.at[5, d], xr.at[5, d], xm),
            ]
        )
    y_up, y_down = (e + 2) % 8, (e + 6) % 8
    other = e + 1 - 2 * core
    upper, lower = pl.ds(0, 512), pl.ds(512, 512)
    def over_y(part_rows, ee, n, to):
        ref = wb.at[part_rows, eighth(ee)]
        return remote(ref, ref, o_s.at[n], o_r.at[n], at(z, x, to))

    w_y = [
        over_y(upper, e, 8, y_up),
        over_y(lower, e, 9, y_down),
        over_y(lower, e, 10, y_up),
        over_y(upper, e, 11, y_down),
        over_y(upper, y_down, 12, y_up),
        over_y(lower, y_up, 13, y_down),
    ]
    w_c = [
        remote(wb.at[:, cols], wb.at[:, cols], o_s.at[14 + i], o_r.at[14 + i], at(z, x, other))
        for i, cols in enumerate(
            (eighth(e), eighth(y_down), eighth(y_up), eighth((e + 4) % 8))
        )
    ]
    w_x[0].wait_recv()
    w_x[2].start()
    w_x[1].wait_recv()
    w_x[3].start()
    for copy in near[0]:
        copy.start()
    local[3].wait()
    w_x[2].wait_recv()
    w_x[3].wait_recv()
    for copy in w_y[:4]:
        copy.start()
    w_c[0].start()
    order = (0, 1, 3, 2)
    for d in (1, 3, 2):
        kv_z[d - 1][0].wait_recv()
        kv_z[d - 1][1].wait_recv()
        for copy in near[d]:
            copy.start()
    wd_copy.wait()
    vec[...] = jnp.broadcast_to(
        jnp.sum(rhs_t(three_rows(head[...], D), wd[...]), axis=0, keepdims=True), (8, 512)
    )
    vec_copy = remote(vec, vec_far, v_s, v_r, partner_w)
    vec_copy.start()
    for d in order:
        near[d][0].wait_recv()
        far[d][0].start()
        near[d][3].wait_recv()
        far[d][1].start()
        if d == 1:
            w_y[0].wait_recv()
            w_y[4].start()
            w_y[1].wait_recv()
            w_y[5].start()
    for d in order:
        near[d][1].wait_recv()
        near[d][2].wait_recv()
        far[d][0].wait_recv()
        far[d][1].wait_recv()
    local[2].wait()
    for d in (1, 3, 2):
        q_z[d - 1].wait_recv()

    own_w, far_w = [], []
    for c in range(2):
        cols = pl.ds(c * 256, 256)
        for i, (hbm, buf) in enumerate(((wg_hbm, wg), (wu_hbm, wu))):
            own_w.append(pltpu.make_async_copy(hbm.at[:, cols], buf.at[c], lsem.at[4 + 2 * c + i]))
            far_w.append(
                remote(hbm.at[:, cols], buf.at[2 + c], w_s.at[2 * c + i], w_r.at[2 * c + i], partner_w)
            )
    for copy in far_w + own_w:
        copy.start()

    bound = len_ref[0, 0]
    second = len_ref[0, 1]
    scale = HEAD_DIM ** (-0.5) * 1.4426950408889634

    def query_step(zq, _):
        q_all = qb[zq]
        stacked = [
            jnp.concatenate(
                [q_all[:, (4 * h + j) * 128 : (4 * h + j + 1) * 128] for j in range(4)], axis=0
            )
            for h in range(2)
        ]
        qpos = (zq * 4 + x) * TOK + lax.broadcasted_iota(jnp.int32, (TOK, 512), 0)
        first = jnp.where(qpos >= bound, bound, 0)

        def key_step(kz, carry):
            kpos = kz * 512 + lax.broadcasted_iota(jnp.int32, (TOK, 512), 1)
            bias = jnp.where(jnp.logical_and(kpos <= qpos, kpos >= first), 0.0, NEG)
            out = []
            for h in range(2):
                m, l, acc = carry[h]
                sc = rhs_t(stacked[h], kb[kz, :, h * 128 : (h + 1) * 128])
                sc = (sc.reshape(4, TOK, 512) + bias[None]).reshape(512, 512)
                mn = jnp.maximum(m, jnp.max(sc, axis=1, keepdims=True))
                p = jnp.exp2((sc - mn) * scale)
                a = jnp.exp2((m - mn) * scale)
                l = a * l + jnp.sum(p, axis=1, keepdims=True)
                acc = a * acc + mm(p.astype(BF16), vb[kz, :, h * 128 : (h + 1) * 128])
                out.append((mn, l, acc))
            return tuple(out)

        start = (
            jnp.full((512, 1), NEG, F32),
            jnp.zeros((512, 1), F32),
            jnp.zeros((512, 128), F32),
        )
        done = lax.fori_loop(0, zq + 1, key_step, (start, start))
        for h in range(2):
            _, l, acc = done[h]
            out = (acc / l).astype(BF16)
            for j in range(4):
                att[zq, :, (4 * h + j) * 128 : (4 * h + j + 1) * 128] = out[j * 128 : (j + 1) * 128]
        return 0

    query_step(z2, 0)
    w_y[2].wait_recv()
    w_y[3].wait_recv()
    w_c[1].start()
    w_c[2].start()
    ids = lax.broadcasted_iota(jnp.int32, (TOK, EXPERTS), 1)
    hot = [ids == routes[:, k : k + 1] for k in range(2)]
    named = jnp.where(jnp.logical_or(hot[0], hot[1]), 1.0, 0.0).astype(BF16)
    earlier = jnp.where(
        lax.broadcasted_iota(jnp.int32, (TOK, TOK), 1) < lax.broadcasted_iota(jnp.int32, (TOK, TOK), 0),
        1.0,
        0.0,
    ).astype(BF16)
    before = mm(earlier, named)
    slot_ids = lax.broadcasted_iota(jnp.int32, (TOK, ROWS), 1)
    slot_hot = []
    for k in range(2):
        rank = jnp.sum(jnp.where(hot[k], before, 0.0), axis=1, keepdims=True).astype(jnp.int32)
        expert = routes[:, k : k + 1]
        slot = jnp.where(
            rank < MAIN, expert * MAIN + rank, EXPERTS * MAIN + expert * 2 + (rank - MAIN)
        )
        slot_hot.append(jnp.where(slot_ids == slot, 1.0, 0.0).astype(BF16))
    slot_any = slot_hot[0] + slot_hot[1]
    tpos = (z * 4 + x) * TOK + lax.broadcasted_iota(jnp.int32, (TOK, 1), 0)
    in_second = tpos >= bound
    own_len = jnp.where(in_second, second, bound).astype(F32)
    tall = lax.broadcasted_iota(jnp.int32, (TOK, REST), 0)
    wide = lax.broadcasted_iota(jnp.int32, (TOK, REST), 1)
    base = (wide // 2) * 16 + (wide % 2) * 8
    picks = [jnp.where(tall == base + kk, 1.0, 0.0).astype(BF16) for kk in range(6)]
    tall_t = lax.broadcasted_iota(jnp.int32, (REST, TOK), 0)
    wide_t = lax.broadcasted_iota(jnp.int32, (REST, TOK), 1)
    base_t = (tall_t // 2) * 16 + (tall_t % 2) * 8
    picks_t = [jnp.where(wide_t == base_t + kk, 1.0, 0.0).astype(BF16) for kk in range(6)]

    rsc = [
        [
            remote(part.at[c, i], rs.at[c, i], rs_s.at[c, i], rs_r.at[c, i], zp if i % 2 == 0 else zm)
            for i in range(6)
        ]
        for c in range(CHUNKS)
    ]

    def project(target, block):
        return mm(att[target], wb[:, block * BLK : (block + 1) * BLK])

    def s1(c):
        for half in range(2):
            part[c, half] = project(z2, 2 * c + half).astype(BF16)
            rsc[c][half].start()

    def s2(c):
        part[c, 2] = project(z1, 2 * c + 1).astype(BF16)
        rsc[c][2].start()
        part[c, 3] = project(z3, 2 * c).astype(BF16)
        rsc[c][3].start()

    def s3(c):
        for half, target in ((0, z1), (1, z3)):
            through = project(target, 2 * c + half)
            rsc[c][half].wait_recv()
            part[c, 4 + half] = (through + rs[c, half].astype(F32)).astype(BF16)
            rsc[c][4 + half].start()

    state = {"square": jnp.zeros((TOK, 1), F32), "logits": jnp.zeros((TOK, EXPERTS), F32)}

    def s4(c):
        sums = []
        for half in range(2):
            span = slice((2 * c + half) * BLK, (2 * c + half + 1) * BLK)
            sums.append(res[:, span].astype(F32) + project(z, 2 * c + half))
        for i in (2, 3, 4, 5):
            rsc[c][i].wait_recv()
        for half, terms in ((0, (3, 4)), (1, (2, 5))):
            span = slice((2 * c + half) * BLK, (2 * c + half + 1) * BLK)
            h = sums[half] + rs[c, terms[0]].astype(F32) + rs[c, terms[1]].astype(F32)
            hid[:, span] = h
            state["square"] = state["square"] + jnp.sum(h * h, axis=1, keepdims=True)
            nrm[:, span] = (h * gain[:, span]).astype(BF16)
        span = slice(c * CW, (c + 1) * CW)
        r_all = router[:, span]
        r_hi = r_all.astype(BF16)
        r_rest = r_all - r_hi.astype(F32)
        r_mid = r_rest.astype(BF16)
        r_low = (r_rest - r_mid.astype(F32)).astype(BF16)
        rows_c = nrm[:, span]
        state["logits"] = (
            state["logits"] + rhs_t(rows_c, r_hi) + rhs_t(rows_c, r_mid) + rhs_t(rows_c, r_low)
        )

    own_slot = 2 * z
    my_rows = pl.ds(pl.multiple_of(e * MAIN, MAIN), MAIN)
    last = CHUNKS - 1
    wide_cols = lambda c: pl.ds(c * CW, CW + (EXT if c == last else 0))
    pack_cols = lambda c: pl.ds(c * 128, 256 if c == last else 128)
    y_copies, keep = [], []
    for c in range(CHUNKS):
        copies = []
        for d in range(1, 8):
            et = (e + d) % 8
            to = at(z, x, et)
            copies.append(
                remote(
                    stage.at[pl.ds(pl.multiple_of(et * MAIN, MAIN), MAIN), wide_cols(c)],
                    xb.at[own_slot, my_rows, wide_cols(c)],
                    y_s.at[c, 0, d - 1],
                    y_r.at[c, 0, d - 1],
                    to,
                )
            )
            copies.append(
                remote(
                    pack.at[et, :, pack_cols(c)],
                    unpack.at[e, :, pack_cols(c)],
                    y_s.at[c, 1, d - 1],
                    y_r.at[c, 1, d - 1],
                    to,
                )
            )
        y_copies.append(copies)
        keep.append(
            [
                pltpu.make_async_copy(
                    stage.at[my_rows, wide_cols(c)],
                    xb.at[own_slot, my_rows, wide_cols(c)],
                    lsem.at[8 + 2 * c],
                ),
                pltpu.make_async_copy(
                    pack.at[e, :, pack_cols(c)], unpack.at[e, :, pack_cols(c)], lsem.at[9 + 2 * c]
                ),
            ]
        )

    def scaled_ext():
        norm_scale = lax.rsqrt(state["square"] * (1.0 / D) + 1e-05)
        logits = state["logits"] * norm_scale
        picked = [jnp.sum(jnp.where(hot[k], logits, 0.0), axis=1, keepdims=True) for k in range(2)]
        gates = [
            1.0 / (1.0 + jnp.exp(picked[1] - picked[0])),
            1.0 / (1.0 + jnp.exp(picked[0] - picked[1])),
        ]
        lanes = lax.broadcasted_iota(jnp.int32, (TOK, EXT), 1)
        s_hi = norm_scale.astype(BF16).astype(F32)
        s_low = norm_scale - s_hi
        scales = jnp.where(lanes == 16, s_hi, jnp.where(lanes == 17, s_low, 0.0)).astype(BF16)
        ext = lhs_t(slot_any, scales)
        bucket = jnp.where(in_second, 8, 0) + e
        for k in range(2):
            weight = (gates[k] / own_len).astype(BF16).astype(F32)
            ext = ext + lhs_t(slot_hot[k], jnp.where(lanes == bucket, weight, 0.0).astype(BF16))
        stage[:, D:] = ext.astype(BF16)

    def send_y(c):
        span = slice(c * CW, (c + 1) * CW)
        stage[:, span] = lhs_t(slot_any, nrm[:, span]).astype(BF16)
        if c == last:
            scaled_ext()
        got = jnp.zeros((TOK, 128), F32)
        for kk in range(6):
            col = c * CW + kk * 128
            got = got + mm(picks[kk], stage[EXPERTS * MAIN :, col : col + 128])
        pack[:, :, c * 128 : (c + 1) * 128] = got.astype(BF16).reshape(EXPERTS, 16, 128)
        if c == last:
            got = mm(picks[0], stage[EXPERTS * MAIN :, D:])
            pack[:, :, (c + 1) * 128 : (c + 2) * 128] = got.astype(BF16).reshape(EXPERTS, 16, 128)
        for copy in y_copies[c] + keep[c]:
            copy.start()

    slot_of = lambda d: 2 * ((z + 4 - d) % 4)
    top, bottom = pl.ds(0, 128), pl.ds(128, ROWS - 128)

    def ring(c, side, s_sem, r_sem):
        cw = wide_cols(c)
        o, a, b = own_slot + side, slot_of(1) + side, slot_of(3) + side
        return [
            remote(xb.at[o, :, cw], xb.at[o, :, cw], s_sem(0), r_sem(0), zp),
            remote(xb.at[o, :, cw], xb.at[o, :, cw], s_sem(1), r_sem(1), zm),
            remote(xb.at[a, top, cw], xb.at[a, top, cw], s_sem(2), r_sem(2), zp),
            remote(xb.at[b, bottom, cw], xb.at[b, bottom, cw], s_sem(3), r_sem(3), zm),
        ]

    zc = [
        ring(c, 0, lambda i, c=c: z_s.at[c, i], lambda i, c=c: z_r.at[c, i]) for c in range(CHUNKS)
    ]
    zd = {
        c: ring(c, 1, lambda i, n=n: zd_s.at[n, i], lambda i, n=n: zd_r.at[n, i])
        for n, c in enumerate(X_FIRST)
    }
    xc = [
        [
            remote(
                xb.at[slot_of(d), :, wide_cols(c)],
                xb.at[slot_of(d) + 1, :, wide_cols(c)],
                x_s.at[c, d],
                x_r.at[c, d],
                partner_t,
            )
            for d in range(1 if c in X_FIRST else 4)
        ]
        for c in range(CHUNKS)
    ]

    def take_y(c):
        for copy in keep[c]:
            copy.wait()
        for copy in y_copies[c]:
            copy.wait_recv()
        flat = unpack[:, :, c * 128 : (c + 1) * 128].reshape(TOK, 128)
        for kk in range(6):
            col = c * CW + kk * 128
            xb[own_slot, EXPERTS * MAIN :, col : col + 128] = mm(picks_t[kk], flat).astype(BF16)
        if c == last:
            flat = unpack[:, :, (c + 1) * 128 : (c + 2) * 128].reshape(TOK, 128)
            xb[own_slot, EXPERTS * MAIN :, D:] = mm(picks_t[0], flat).astype(BF16)
        xc[c][0].start()
        zc[c][0].start()
        zc[c][1].start()

    def pass_x(c):
        xc[c][0].wait_recv()
        zd[c][0].start()
        zd[c][1].start()

    def pass_z(c):
        zc[c][0].wait_recv()
        zc[c][2].start()
        zc[c][1].wait_recv()
        zc[c][3].start()
        if c not in X_FIRST:
            xc[c][1].start()
            xc[c][3].start()

    def pass_zd(c):
        zd[c][0].wait_recv()
        zd[c][2].start()
        zd[c][1].wait_recv()
        zd[c][3].start()

    def pass_far(c):
        zc[c][2].wait_recv()
        zc[c][3].wait_recv()
        if c not in X_FIRST:
            xc[c][2].start()

    def experts(slot, low, high):
        def chunk_step(c, _):
            rows_x = xb[slot, :, :D]
            ext = xb[slot, :, D:]
            row_scale = ext[:, 16:17].astype(F32) + ext[:, 17:18].astype(F32)
            gate = mm(rows_x, wg[c]) * row_scale
            up = mm(rows_x, wu[c]) * row_scale
            act = (gate / (1.0 + jnp.exp(-gate)) * up).astype(BF16)
            hs[c] = hs[c] + lhs_t(ext, act)
            return 0

        lax.fori_loop(low, high, chunk_step, 0)

    def last_products(slot, start, stop):
        span = slice(start * CW, stop * CW)

        def chunk_step(c, _):
            rows_x = xb[slot, :, span]
            gate = mm(rows_x, wg[c, span])
            up = mm(rows_x, wu[c, span])
            if start:
                gate = gate + kept[0, c]
                up = up + kept[1, c]
            if stop < CHUNKS:
                kept[0, c] = gate
                kept[1, c] = up
            else:
                ext = xb[slot, :, D:]
                row_scale = ext[:, 16:17].astype(F32) + ext[:, 17:18].astype(F32)
                gate = gate * row_scale
                act = (gate / (1.0 + jnp.exp(-gate)) * (up * row_scale)).astype(BF16)
                hs[c] = hs[c] + lhs_t(ext, act)
            return 0

        lax.fori_loop(0, 4, chunk_step, 0)

    w_y[4].wait_recv()
    w_y[5].wait_recv()
    w_c[3].start()
    for copy in w_c:
        copy.wait_recv()
    for c in range(CHUNKS):
        s1(c)
    lax.fori_loop(0, 2, lambda i, _: query_step((z1 + 2 * i) % 4, _), 0)
    s2(0)
    s3(0)
    s2(1)
    s3(1)
    query_step(z, 0)
    s2(2)
    s3(2)
    s4(0)
    send_y(0)
    s2(3)
    s4(1)
    send_y(1)
    take_y(0)
    s3(3)
    s4(2)
    send_y(2)
    take_y(1)
    s4(3)
    send_y(3)
    pass_z(0)
    take_y(2)
    pass_x(1)
    inv = 1.0 / own_len
    pool[...] = jnp.zeros_like(pool)
    pool[0:1] = jnp.sum(hid[...] * jnp.where(in_second, 0.0, inv), axis=0, keepdims=True)
    pool[1:2] = jnp.sum(hid[...] * jnp.where(in_second, inv, 0.0), axis=0, keepdims=True)
    hs[...] = jnp.zeros_like(hs)
    take_y(3)
    pass_z(1)
    for copy in own_w:
        copy.wait()
    experts(own_slot, 0, 2)
    pass_z(2)
    pass_zd(1)
    for c in range(CHUNKS):
        if c not in X_FIRST:
            xc[c][0].wait_recv()
    experts(own_slot + 1, 0, 2)
    pass_z(3)
    for copy in far_w:
        copy.wait_recv()
    pass_far(0)
    experts(own_slot, 2, 4)
    experts(own_slot + 1, 2, 4)
    pass_far(1)
    experts(slot_of(1), 0, 4)
    pass_far(2)
    pass_far(3)
    experts(slot_of(3), 0, 4)
    for d in (1, 3):
        for c in range(CHUNKS):
            if c not in X_FIRST:
                xc[c][d].wait_recv()
        experts(slot_of(d) + 1, 0, 4)
    experts(slot_of(2), 0, 4)
    zd[1][2].wait_recv()
    zd[1][3].wait_recv()
    xc[0][2].wait_recv()
    last_products(slot_of(2) + 1, 0, 2)
    xc[2][2].wait_recv()
    last_products(slot_of(2) + 1, 2, 3)
    xc[3][2].wait_recv()
    last_products(slot_of(2) + 1, 3, 4)

    home = remote(hs.at[pl.ds(2, 2), pl.ds(0, 16)], hr, h_s, h_r, partner_w)
    home.start()
    vec_copy.wait_recv()
    s = z * 4 + x
    exp_peers = [(s, (e + d) % 8) for d in range(1, 8)]
    seq_peers = [((s + d) % 16, e) for d in range(1, 16)]

    def all_sum(mine, got_exp, total, got_seq, es, er, qs, qr):
        copies = [
            remote(mine, got_exp.at[i], es.at[i], er.at[i], to) for i, to in enumerate(exp_peers)
        ]
        for copy in copies:
            copy.start()
        acc = mine[...]
        for i, copy in enumerate(copies):
            copy.wait_recv()
            acc = acc + got_exp[i]
        total[...] = acc
        more = [
            remote(total, got_seq.at[i], qs.at[i], qr.at[i], to) for i, to in enumerate(seq_peers)
        ]
        for copy in more:
            copy.start()
        for i, copy in enumerate(more):
            copy.wait_recv()
            acc = acc + got_seq[i]
        return acc, copies + more

    part_r = jnp.zeros((16, 1), F32)
    for c in range(2):
        span = slice(c * 256, (c + 1) * 256)
        part_r = part_r + jnp.sum(
            hs[c, 0:16] * vec[0:1, span] + hs[2 + c, 0:16] * vec_far[0:1, span], axis=1, keepdims=True
        )
    own = jnp.sum(pool[...] * head[...], axis=1, keepdims=True)
    group = lax.broadcasted_iota(jnp.int32, (8, 128), 0)
    r_mine[0:8] = part_r[0:8] + jnp.where(group == e, own[0:1], 0.0)
    r_mine[8:16] = part_r[8:16] + jnp.where(group == e, own[1:2], 0.0)
    rewards, sent = all_sum(r_mine, r_exp, r_sum, r_seq, re_s, re_r, rq_s, rq_r)

    home.wait_recv()
    hsv = jnp.concatenate([hs[c, 0:16] + hr[c] for c in range(2)], axis=1)
    r0, r1 = rewards[0:8], rewards[8:16]
    lane = lax.broadcasted_iota(jnp.int32, (8, 128), 1)
    rew_out[...] = jnp.where(lane == 0, r0, r1)[:, :2]
    named_pair = pairs[...]
    value = jnp.where(named_pair == 0, r0, r1)
    margin = value - pltpu.roll(value, 127, 1)
    real = jnp.logical_and(lane % 2 == 0, lane < 8)
    loss = jnp.maximum(-margin, 0.0) + jnp.log1p(jnp.exp(-jnp.abs(margin)))
    loss = jnp.sum(jnp.where(real, loss, 0.0), axis=1, keepdims=True)
    loss_out[...] = jnp.sum(loss, axis=0, keepdims=True) * (1.0 / 32.0)
    factor = jnp.where(real, -1.0 / (1.0 + jnp.exp(margin)) * (1.0 / 32.0), 0.0)
    factor = factor - pltpu.roll(factor, 1, 1)
    rg0 = jnp.sum(jnp.where(named_pair == 0, factor, 0.0), axis=1, keepdims=True)
    rg1 = jnp.sum(jnp.where(named_pair == 1, factor, 0.0), axis=1, keepdims=True)
    weighted = jnp.sum(hsv[0:8] * rg0 + hsv[8:16] * rg1, axis=0, keepdims=True)
    wt_out[...] = weighted
    moved = jnp.sum(mm(three_rows(weighted, 512), wd[...]), axis=0, keepdims=True)
    me_row = lax.broadcasted_iota(jnp.int32, (8, 1), 0) == e
    own0 = jnp.sum(jnp.where(me_row, rg0, 0.0), axis=0, keepdims=True)
    own1 = jnp.sum(jnp.where(me_row, rg1, 0.0), axis=0, keepdims=True)
    grad = moved + own0 * pool[0:1] + own1 * pool[1:2]
    for i in range(24):
        g_mine[i : i + 1] = grad[:, i * 128 : (i + 1) * 128]
    gh_out[...], more = all_sum(g_mine, g_exp, g_sum, g_seq, ge_s, ge_r, gq_s, gq_r)

    started = [home, vec_copy, *sent, *more, *q_z, *w_x, *w_y, *w_c, *far_w]
    for group in (*kv_z, *near, *far, *rsc, *y_copies, *zc, *zd.values(), *xc):
        started.extend(group)
    for copy in started:
        copy.wait_send()


def layer(lengths, q, k, v, op, res, gain, router_t, routes, w_gate, w_up, w_down, head, pairs):
    vmem = pl.BlockSpec(memory_space=pltpu.VMEM)
    hbm = pl.BlockSpec(memory_space=pl.ANY)
    dma = pltpu.SemaphoreType.DMA
    return pl.pallas_call(
        layer_kernel,
        out_shape=(
            jax.ShapeDtypeStruct((EXPERTS, SEQS), F32),
            jax.ShapeDtypeStruct((1, 1), F32),
            jax.ShapeDtypeStruct((24, 128), F32),
            jax.ShapeDtypeStruct((1, 512), F32),
        ),
        in_specs=[pl.BlockSpec(memory_space=pltpu.SMEM)] + [hbm] * 4 + [vmem] * 4 + [hbm] * 3 + [vmem] * 2,
        out_specs=(vmem,) * 4,
        scratch_shapes=[
            pltpu.VMEM((4, TOK, 1024), BF16),
            pltpu.VMEM((4, 512, 256), BF16),
            pltpu.VMEM((4, 512, 256), BF16),
            pltpu.VMEM((4, TOK, 1024), BF16),
            pltpu.VMEM((1024, D), BF16),
            pltpu.VMEM((CHUNKS, 6, TOK, BLK), BF16),
            pltpu.VMEM((CHUNKS, 6, TOK, BLK), BF16),
            pltpu.VMEM((TOK, D), F32),
            pltpu.VMEM((TOK, D), BF16),
            pltpu.VMEM((ROWS, WIDE), BF16),
            pltpu.VMEM((EXPERTS, 16, 128 * (CHUNKS + 1)), BF16),
            pltpu.VMEM((EXPERTS, 16, 128 * (CHUNKS + 1)), BF16),
            pltpu.VMEM((8, ROWS, WIDE), BF16),
            pltpu.VMEM((4, D, 256), BF16),
            pltpu.VMEM((4, D, 256), BF16),
            pltpu.VMEM((4, EXT, 256), F32),
            pltpu.VMEM((2, 16, 256), F32),
            dma((10 + 2 * CHUNKS,)),
            dma((3, 3)), dma((3, 3)),
            dma((6, 4)), dma((6, 4)),
            dma((19,)), dma((19,)),
            dma((CHUNKS, 6)), dma((CHUNKS, 6)),
            dma((4,)), dma((4,)),
            dma((CHUNKS, 2, 7)), dma((CHUNKS, 2, 7)),
            dma((CHUNKS, 4)), dma((CHUNKS, 4)),
            dma((max(1, len(X_FIRST)), 4)), dma((max(1, len(X_FIRST)), 4)),
            dma((CHUNKS, 4)), dma((CHUNKS, 4)),
            dma, dma,
            pltpu.VMEM((512, D), BF16), pltpu.VMEM((8, 512), F32), pltpu.VMEM((8, 512), F32), dma, dma,
            pltpu.VMEM((2, 4, ROWS, 256), F32), pltpu.VMEM((8, D), F32),
            pltpu.VMEM((16, 128), F32), pltpu.VMEM((7, 16, 128), F32),
            pltpu.VMEM((16, 128), F32), pltpu.VMEM((15, 16, 128), F32),
            pltpu.VMEM((24, 128), F32), pltpu.VMEM((7, 24, 128), F32),
            pltpu.VMEM((24, 128), F32), pltpu.VMEM((15, 24, 128), F32),
            dma((7,)), dma((7,)), dma((15,)), dma((15,)),
            dma((7,)), dma((7,)), dma((15,)), dma((15,)),
        ],
        compiler_params=pltpu.CompilerParams(
            collective_id=0, has_side_effects=True, vmem_limit_bytes=VMEM_LIMIT
        ),
        cost_estimate=pl.CostEstimate(
            flops=36_000_000_000, bytes_accessed=24_000_000, transcendentals=8_000_000
        ),
        name="layer",
    )(lengths, q, k, v, op, res, gain, router_t, routes, w_gate, w_up, w_down, head, pairs)


def per_device(
    query_states, key_states, value_states, residual, out_proj, norm_gain, router,
    w_gate, w_up, w_down, reward_head, lengths, routes, pair_list,
):
    pairs = jnp.pad(pair_list.reshape(8, 8), ((0, 0), (0, 120)))
    rewards, loss, gh, wt = layer(
        lengths, query_states[0], key_states[0], value_states[0], out_proj, residual[0],
        norm_gain[None, :], router.T, routes[0], w_gate[0], w_up[0], w_down[0],
        reward_head[None, :], pairs,
    )
    grad_down = (wt[0][:, None] * reward_head[None, :]).astype(BF16)[None]
    return rewards, loss.reshape(()), gh.reshape(-1), grad_down


def solution(mesh):
    placed = (
        P("exp", "seq", None), P("exp", "seq", None), P("exp", "seq", None), P("exp", "seq", None),
        P("seq", None), P(), P(), P("exp", None, "seq"), P("exp", None, "seq"),
        P("exp", "seq", None), P(), P("exp", None), P("exp", "seq", None), P(),
    )
    return jax.shard_map(
        per_device,
        mesh=mesh,
        in_specs=placed,
        out_specs=(P(), P(), P(), P("exp", "seq", None)),
        check_vma=False,
    )
```
